32 devices in a mesh: lang: 4 (over z), shard: 8 (over y, x, core).
Axes of the slice: x: 2, y: 2, z: 4, core: 2. Of those that a mesh axis runs over, the one named last changes fastest.
Arguments:
- memory: bfloat16 [32, 16, 4096], P(('lang', 'shard')), may hold values from -6 to 6
- lang_id: int32 [32], P(('lang', 'shard')), may hold values from 0 to 3, as said below
- src_len: int32 [32], P(('lang', 'shard')), may hold values from 4 to 16
- tgt_len: int32 [32], P(('lang', 'shard')), may hold values from 32 to 128
- queries: bfloat16 [4, 16, 128, 4096], P('lang', 'shard'), may hold values from -64 to 64
- key_weight: bfloat16 [4, 4096, 4096], P('lang', None, 'shard'), may hold values from -1 to 1
- value_weight: bfloat16 [4, 4096, 4096], P('lang', None, 'shard'), may hold values from -0.09375 to 0.09375
- grad_context: bfloat16 [4, 16, 128, 4096], P('lang', 'shard'), may hold values from -6 to 6
Outputs:
- context: bfloat16 [4, 16, 128, 4096], P('lang', 'shard')
- grad_queries: bfloat16 [4, 16, 128, 4096], P('lang', 'shard')
- grad_memory: bfloat16 [32, 16, 4096], P(('lang', 'shard'))
- grad_key_weight: bfloat16 [4, 4096, 4096], P('lang', None, 'shard')
- grad_value_weight: bfloat16 [4, 4096, 4096], P('lang', None, 'shard')
The draws below stay inside these ranges and needn't reach their ends.
Inputs may be any that keep to these rules, and one draw needn't show every extreme that they name: `lang_id`: among the 4 sentences of one column b (indices a * 8 + b), no language is named more than 2 times, and in every column some language is named exactly 2 times.
All inputs are finite; a program needn't handle non-finite values.
Results may differ from the reference program's by a relative error of at most 0.025.
The reference program's roundings to bfloat16 on the way count: a program that leaves them out, or rounds other values in their place, can miss the bound.
Values may be sent and summed in bfloat16 or wider, within the bound.
A program may use at most 128 MiB of HBM per device.

```python
import jax
import jax.numpy as jnp
from jax import lax

D = 4096
HEADS = 32
HEAD = 128
LT = 128
LS = 16
MOST = 2
HK = 4096
LANGS = 4
SLOTS = 16
SENTS = 32
N_SHARD = 8


def draw_lang_id(key, part):
    key = jax.random.fold_in(key, 11)
    columns = SENTS // LANGS
    key_favour, key_first, key_second, key_sets, key_order = jax.random.split(key, 5)
    favoured = jax.random.permutation(key_favour, LANGS)
    first_pick = jax.random.randint(key_first, (columns,), 0, LANGS)
    second_pick = jax.random.randint(key_second, (columns,), 0, LANGS)
    pair_lang = favoured[jnp.minimum(first_pick, second_pick)]

    def shuffle_doubled(row_key):
        return jax.random.permutation(row_key, 2 * LANGS)

    def shuffle_column(row_key):
        return jax.random.permutation(row_key, LANGS)
    shuffles = jax.vmap(shuffle_doubled)(jax.random.split(key_sets, columns))
    language = shuffles // 2
    ordering = jnp.argsort(shuffles + jnp.where(language == pair_lang[:, None], 2 * LANGS, 0), axis=1, stable=True)
    chosen = jnp.take_along_axis(language, ordering, axis=1)[:, :LANGS - 2]
    column_ids = jnp.concatenate([pair_lang[:, None], pair_lang[:, None], chosen], axis=1)
    placing = jax.vmap(shuffle_column)(jax.random.split(key_order, columns))
    column_ids = jnp.take_along_axis(column_ids, placing, axis=1)
    return column_ids.T.reshape(SENTS).astype(jnp.int32)


def draw_src_len(key, part):
    key = jax.random.fold_in(key, 12)
    lengths = jax.random.randint(key, (SENTS,), max(1, LS // 4), LS + 1)
    return lengths.at[0].set(LS).astype(jnp.int32)


def draw_tgt_len(key, part):
    key = jax.random.fold_in(key, 13)
    lengths = jax.random.randint(key, (SENTS,), max(1, LT // 4), LT + 1)
    return lengths.at[0].set(LT).astype(jnp.int32)


def draw_queries(key, part):
    key = jax.random.fold_in(key, 14)
    key_base = jax.random.fold_in(key, 0)
    values = jax.random.truncated_normal(key_base, -4.0, 4.0, (LANGS, SLOTS, LT, HK), jnp.float32)
    return values.astype(jnp.bfloat16)


def draw_memory(key, part):
    key = jax.random.fold_in(key, 15)
    values = jax.random.truncated_normal(key, -6.0, 6.0, (SENTS, LS, D), jnp.float32)
    return values.astype(jnp.bfloat16)


def draw_key_weight(key, part):
    key = jax.random.fold_in(key, 16)
    weights = jax.random.truncated_normal(key, -4.0, 4.0, (LANGS, D, HK), jnp.float32) * D ** (-0.5)
    return weights.astype(jnp.bfloat16)


def level_of(stream_key, dims, pieces, low, top_value):
    factor_of = 1.0
    for dim, shards_of in pieces:
        draws = jax.random.uniform(jax.random.fold_in(jax.random.fold_in(stream_key, 6), dim), (shards_of,), jnp.float32, low / len(pieces), top_value / len(pieces))
        factor_of = factor_of * jnp.repeat(jnp.exp(draws), dims[dim] // shards_of).reshape((-1,) + (1,) * (len(dims) - 1 - dim))
    return factor_of


def normal_values(own_key, extent, width, limit, cuts=(), held_as=jnp.bfloat16):
    result = jax.random.normal(own_key, extent, jnp.float32) * width
    if len(cuts) > 0:
        result = level_of(own_key, extent, cuts, -0.22, 0.18) * result
    return jnp.clip(result, min=-limit, max=limit).astype(held_as)


def setup_inputs(seed: int = 0) -> dict:
    seeds = jax.random.split(jax.random.key(seed), 9)
    memory = draw_memory(jax.random.fold_in(seeds[8], 71), 0)
    lang_id = draw_lang_id(jax.random.fold_in(seeds[8], 71), 0)
    src_len = draw_src_len(jax.random.fold_in(seeds[8], 71), 0)
    tgt_len = draw_tgt_len(jax.random.fold_in(seeds[8], 71), 0)
    queries = draw_queries(jax.random.fold_in(seeds[8], 71), 0)
    key_weight = draw_key_weight(jax.random.fold_in(seeds[8], 71), 0)
    value_weight = normal_values(seeds[6], (LANGS, D, HK), D ** -0.5, 0.09375, ((0, 4), (2, 8)))
    grad_context = normal_values(seeds[7], (LANGS, SLOTS, LT, HK), 1.0, 6.0, ((0, 4), (1, 8)))
    return dict(memory=memory, lang_id=lang_id, src_len=src_len, tgt_len=tgt_len, queries=queries, key_weight=key_weight, value_weight=value_weight, grad_context=grad_context)


masked_score = -1e30


def route_slots(lang_id):
    columns = SENTS // LANGS
    grid = lang_id.reshape(LANGS, columns)
    matching = grid[:, None, :] == grid[None, :, :]
    earlier = jnp.arange(LANGS)[None, :] < jnp.arange(LANGS)[:, None]
    position = jnp.sum(jnp.where(matching & earlier[:, :, None], 1, 0), axis=1).astype(jnp.int32)
    slot = jnp.arange(columns, dtype=jnp.int32)[None, :] * MOST + position
    return slot.reshape(SENTS).astype(jnp.int32)


def attend(queries, key_rows, value_rows, grad_ctx, src_slot, tgt_slot):
    scaling = HEAD ** -0.5
    query_f = queries.astype(jnp.float32)
    key_f = key_rows.astype(jnp.float32)
    value_f = value_rows.astype(jnp.float32)
    scores = jnp.einsum("nqhe,nkhe->nhqk", query_f, key_f) * scaling
    key_valid = jnp.arange(LS)[None, :] < jnp.maximum(src_slot, 1)[:, None]
    scores = jnp.where(key_valid[:, None, None, :], scores, masked_score)
    row_max = jnp.max(scores, axis=-1, keepdims=True)
    shifted = jnp.exp(scores - row_max)
    attention = shifted / jnp.sum(shifted, axis=-1, keepdims=True)
    attention_bf = attention.astype(jnp.bfloat16).astype(jnp.float32)
    row_valid = (jnp.arange(LT)[None, :] < tgt_slot[:, None])[:, :, None, None]
    context = jnp.einsum("nhqk,nkhe->nqhe", attention_bf, value_f)
    context = jnp.where(row_valid, context, 0.0).astype(jnp.bfloat16)
    grad_masked = jnp.where(row_valid, grad_ctx.astype(jnp.float32), 0.0)
    grad_values = jnp.einsum("nhqk,nqhe->nkhe", attention_bf, grad_masked).astype(jnp.bfloat16)
    grad_attention = jnp.einsum("nqhe,nkhe->nhqk", grad_masked, value_f)
    row_dot = jnp.sum(attention * grad_attention, axis=-1, keepdims=True)
    grad_scores = (attention * (grad_attention - row_dot)).astype(jnp.bfloat16).astype(jnp.float32)
    grad_queries = (jnp.einsum("nhqk,nkhe->nqhe", grad_scores, key_f) * scaling).astype(jnp.bfloat16)
    grad_keys = (jnp.einsum("nhqk,nqhe->nkhe", grad_scores, query_f) * scaling).astype(jnp.bfloat16)
    return context, grad_queries, grad_keys, grad_values


def one_language(inputs):
    routed, src_slot, tgt_slot, queries, key_weight, value_weight, grad_context = inputs
    flattened = routed.reshape(SLOTS * LS, D)
    key_rows = jnp.dot(flattened, key_weight, preferred_element_type=jnp.float32).astype(jnp.bfloat16)
    value_rows = jnp.dot(flattened, value_weight, preferred_element_type=jnp.float32).astype(jnp.bfloat16)
    source_shape = (SLOTS, LS, HEADS, HEAD)
    target_shape = (SLOTS, LT, HEADS, HEAD)
    context, grad_queries, grad_keys, grad_values = attend(
        queries.reshape(target_shape), key_rows.reshape(source_shape), value_rows.reshape(source_shape),
        grad_context.reshape(target_shape), src_slot, tgt_slot)
    grad_keys = grad_keys.reshape(SLOTS * LS, HK)
    grad_values = grad_values.reshape(SLOTS * LS, HK)
    grad_key_weight = jnp.dot(flattened.T, grad_keys, preferred_element_type=jnp.float32).astype(jnp.bfloat16)
    grad_value_weight = jnp.dot(flattened.T, grad_values, preferred_element_type=jnp.float32).astype(jnp.bfloat16)
    group_cols = HK // N_SHARD

    def add_group(running, group_index):
        first_col = (group_index * group_cols).astype(jnp.int32)
        key_part = lax.dynamic_slice_in_dim(grad_keys, first_col, group_cols, 1)
        value_part = lax.dynamic_slice_in_dim(grad_values, first_col, group_cols, 1)
        key_cols = lax.dynamic_slice_in_dim(key_weight, first_col, group_cols, 1)
        value_cols = lax.dynamic_slice_in_dim(value_weight, first_col, group_cols, 1)
        partial_term = jnp.dot(key_part, key_cols.T, preferred_element_type=jnp.float32)
        partial_term = partial_term + jnp.dot(value_part, value_cols.T, preferred_element_type=jnp.float32)
        rounded = lax.optimization_barrier(partial_term.astype(jnp.bfloat16))
        return running + rounded.astype(jnp.float32), None

    start_sum = jnp.zeros((SLOTS * LS, D), jnp.float32)
    routed_grad, _ = lax.scan(add_group, start_sum, jnp.arange(N_SHARD, dtype=jnp.int32))
    routed_grad = routed_grad.astype(jnp.bfloat16).reshape(SLOTS, LS, D)
    return (context.reshape(SLOTS, LT, HK), grad_queries.reshape(SLOTS, LT, HK), routed_grad,
            grad_key_weight, grad_value_weight)


def reference(memory, lang_id, src_len, tgt_len, queries, key_weight, value_weight, grad_context):
    slot = route_slots(lang_id)
    routed = jnp.zeros((LANGS, SLOTS, LS, D), jnp.bfloat16).at[lang_id, slot].set(memory)
    src_slot = jnp.zeros((LANGS, SLOTS), jnp.int32).at[lang_id, slot].set(src_len)
    tgt_slot = jnp.zeros((LANGS, SLOTS), jnp.int32).at[lang_id, slot].set(tgt_len)
    context, grad_queries, routed_grad, grad_key_weight, grad_value_weight = lax.map(
        one_language, (routed, src_slot, tgt_slot, queries, key_weight, value_weight, grad_context))
    grad_memory = routed_grad[lang_id, slot]
    return context, grad_queries, grad_memory, grad_key_weight, grad_value_weight
```

```python
import jax
import jax.numpy as jnp
from jax import lax
from jax.sharding import PartitionSpec as P

HEAD = 128


masked_score = -1e30


def attend(queries, key_rows, value_rows, grad_ctx, src_slot, tgt_slot):
    scaling = queries.shape[-1] ** (-0.5)
    source_rows = key_rows.shape[1]
    target_rows = queries.shape[1]
    scores = (
        jnp.einsum("nqhe,nkhe->nhqk", queries, key_rows, preferred_element_type=jnp.float32)
        * scaling
    )
    key_valid = jnp.arange(source_rows)[None, :] < jnp.maximum(src_slot, 1)[:, None]
    scores = jnp.where(key_valid[:, None, None, :], scores, masked_score)
    row_max = jnp.max(scores, axis=-1, keepdims=True)
    shifted = jnp.exp(scores - row_max)
    attention = shifted / jnp.sum(shifted, axis=-1, keepdims=True)
    attention_bf = attention.astype(jnp.bfloat16)
    row_valid = (jnp.arange(target_rows)[None, :] < tgt_slot[:, None])[:, :, None, None]
    context = jnp.einsum(
        "nhqk,nkhe->nqhe", attention_bf, value_rows, preferred_element_type=jnp.float32
    )
    context = jnp.where(row_valid, context, 0.0).astype(jnp.bfloat16)
    grad_masked = jnp.where(row_valid, grad_ctx, jnp.zeros_like(grad_ctx))
    grad_values = jnp.einsum(
        "nhqk,nqhe->nkhe", attention_bf, grad_masked, preferred_element_type=jnp.float32
    ).astype(jnp.bfloat16)
    grad_attention = jnp.einsum(
        "nqhe,nkhe->nhqk", grad_masked, value_rows, preferred_element_type=jnp.float32
    )
    row_dot = jnp.sum(attention * grad_attention, axis=-1, keepdims=True)
    grad_scores = (attention * (grad_attention - row_dot)).astype(jnp.bfloat16)
    grad_queries = (
        jnp.einsum("nhqk,nkhe->nqhe", grad_scores, key_rows, preferred_element_type=jnp.float32)
        * scaling
    ).astype(jnp.bfloat16)
    grad_keys = (
        jnp.einsum("nhqk,nqhe->nkhe", grad_scores, queries, preferred_element_type=jnp.float32)
        * scaling
    ).astype(jnp.bfloat16)
    return (context, grad_queries, grad_keys, grad_values)


def local(memory, lang_id, src_len, tgt_len, queries, key_weight, value_weight, grad_context):
    lang_count = lax.axis_size("lang")
    shard_count = lax.axis_size("shard")
    lang_index = lax.axis_index("lang")
    column_mem, column_ids, column_src, column_tgt = (
        lax.all_gather(memory, "lang", axis=0, tiled=True),
        lax.all_gather(lang_id, "lang", axis=0, tiled=True),
        lax.all_gather(src_len, "lang", axis=0, tiled=True),
        lax.all_gather(tgt_len, "lang", axis=0, tiled=True),
    )
    slots_dev = queries.shape[1]
    target_rows = queries.shape[2]
    source_rows = memory.shape[1]
    model_width = memory.shape[2]
    head_cols = key_weight.shape[2]
    matching = column_ids[:, None] == column_ids[None, :]
    earlier = jnp.arange(lang_count)[None, :] < jnp.arange(lang_count)[:, None]
    position = jnp.sum(jnp.where(matching & earlier, 1, 0), axis=1).astype(jnp.int32)
    selected = (column_ids[None, :] == lang_index) & (
        position[None, :] == jnp.arange(slots_dev)[:, None]
    )
    routed = jnp.einsum(
        "rj,jsd->rsd", selected.astype(jnp.bfloat16), column_mem, preferred_element_type=jnp.float32
    ).astype(jnp.bfloat16)
    own_src = jnp.sum(jnp.where(selected, column_src[None, :], 0), axis=1).astype(jnp.int32)
    own_tgt = jnp.sum(jnp.where(selected, column_tgt[None, :], 0), axis=1).astype(jnp.int32)
    key_local = key_weight[0]
    value_local = value_weight[0]
    group_rows = lax.all_gather(routed, "shard", axis=0, tiled=True)
    flattened = group_rows.reshape(-1, model_width)
    key_part = jnp.dot(flattened, key_local, preferred_element_type=jnp.float32).astype(
        jnp.bfloat16
    )
    value_part = jnp.dot(flattened, value_local, preferred_element_type=jnp.float32).astype(
        jnp.bfloat16
    )
    joined = jnp.concatenate([key_part, value_part], axis=1)
    projected = joined.reshape(group_rows.shape[0], source_rows, 2 * head_cols)
    key_rows = projected[:, :, :head_cols]
    value_rows = projected[:, :, head_cols:]
    total_slots = key_rows.shape[0]
    local_heads = head_cols // HEAD
    outgoing = projected.reshape(total_slots * source_rows, 1, 2 * head_cols)
    arrived = lax.all_to_all(outgoing, "shard", split_axis=0, concat_axis=1, tiled=True)
    arrived = arrived.reshape(slots_dev, source_rows, shard_count, 2 * head_cols)
    target_shape = (slots_dev, target_rows, shard_count * local_heads, HEAD)
    source_shape = (slots_dev, source_rows, shard_count * local_heads, HEAD)
    context, grad_queries, grad_keys, grad_values = attend(
        queries[0].reshape(target_shape),
        arrived[..., :head_cols].reshape(source_shape),
        arrived[..., head_cols:].reshape(source_shape),
        grad_context[0].reshape(target_shape),
        own_src,
        own_tgt,
    )
    context = context.reshape(1, slots_dev, target_rows, shard_count * head_cols)
    grad_queries = grad_queries.reshape(1, slots_dev, target_rows, shard_count * head_cols)
    back_shape = (slots_dev * source_rows, shard_count, head_cols)
    back = jnp.concatenate(
        [grad_keys.reshape(back_shape), grad_values.reshape(back_shape)], axis=2
    )
    back = lax.all_to_all(back, "shard", split_axis=1, concat_axis=0, tiled=True)
    back = back.reshape(total_slots * source_rows, 2 * head_cols)
    key_part = back[:, :head_cols]
    value_part = back[:, head_cols:]
    grad_keys = key_part
    grad_values = value_part
    contract = (((1,), (1,)), ((), ()))
    summed = lax.dot_general(key_part, key_local, contract, preferred_element_type=jnp.float32)
    summed = summed + lax.dot_general(
        value_part, value_local, contract, preferred_element_type=jnp.float32
    )
    slot_grads = lax.psum_scatter(
        summed.reshape(lax.axis_size("shard") * slots_dev, source_rows, model_width).astype(
            jnp.bfloat16
        ),
        "shard",
        scatter_dimension=0,
        tiled=True,
    )
    transpose_contract = (((0,), (0,)), ((), ()))
    flattened = group_rows.reshape(-1, model_width)
    grad_key_local = lax.dot_general(
        flattened,
        grad_keys.reshape(-1, head_cols),
        transpose_contract,
        preferred_element_type=jnp.float32,
    )
    grad_value_local = lax.dot_general(
        flattened,
        grad_values.reshape(-1, head_cols),
        transpose_contract,
        preferred_element_type=jnp.float32,
    )
    returned = lax.all_gather(slot_grads, "lang", axis=0, tiled=True)
    own_index = lang_id[0] * slots_dev + position[lang_index]
    grad_memory = lax.dynamic_slice_in_dim(returned, own_index, 1, 0)
    return (
        context,
        grad_queries,
        grad_memory,
        grad_key_local.astype(jnp.bfloat16)[None],
        grad_value_local.astype(jnp.bfloat16)[None],
    )


def solution(mesh):
    return jax.shard_map(
        local,
        mesh=mesh,
        in_specs=(
            P(("lang", "shard"), None, None),
            P(("lang", "shard")),
            P(("lang", "shard")),
            P(("lang", "shard")),
            P("lang", "shard", None, None),
            P("lang", None, "shard"),
            P("lang", None, "shard"),
            P("lang", "shard", None, None),
        ),
        out_specs=(
            P("lang", "shard", None, None),
            P("lang", "shard", None, None),
            P(("lang", "shard"), None, None),
            P("lang", None, "shard"),
            P("lang", None, "shard"),
        ),
        check_vma=False,
    )
```

```python
import functools

import jax
import jax.numpy as jnp
from jax import lax
from jax.experimental import pallas as pl
from jax.experimental.pallas import tpu as pltpu
from jax.sharding import PartitionSpec as P

HEAD = 128
CHUNKS = 4
VMEM_BYTES = 50 * 1024 * 1024

masked_score = -1e30
MESH = pl.DeviceIdType.MESH
F32 = jnp.float32
BF16 = jnp.bfloat16


def remote(src, dst, send_sem, recv_sem, device):
    return pltpu.make_async_remote_copy(
        src_ref=src,
        dst_ref=dst,
        send_sem=send_sem,
        recv_sem=recv_sem,
        device_id=device,
        device_id_type=MESH,
    )


def enter(lang, shard, langs, shards):
    barrier = pltpu.get_barrier_semaphore()
    for step in range(1, langs):
        pl.semaphore_signal(
            barrier, inc=1, device_id=(lax.rem(lang + step, langs), shard), device_id_type=MESH
        )
    for step in range(1, shards):
        pl.semaphore_signal(
            barrier, inc=1, device_id=(lang, lax.rem(shard + step, shards)), device_id_type=MESH
        )
    pl.semaphore_wait(barrier, langs + shards - 2)


def selection(facts, lang, langs, slots):
    ids = [facts[j, 0:1, 0:1] for j in range(langs)]
    chosen = [[None] * langs for _ in range(slots)]
    for j in range(langs):
        rank = jnp.zeros((1, 1), jnp.int32)
        for k in range(j):
            rank = rank + jnp.where(ids[k] == ids[j], 1, 0)
        here = ids[j] == lang
        for r in range(slots):
            chosen[r][j] = jnp.where(here & (rank == r), 1, 0)
    return chosen


def route_kernel(
    langs, shards, slots,
    memory, facts_in, key_weight, value_weight,
    group, rows_out, facts, lengths,
    column, weights, total, outgoing,
    weight_sem, fact_send, fact_recv, z_send, z_recv,
    p_send, p_recv, s_send, s_recv, a_send, a_recv,
):
    lang = lax.axis_index("lang")
    shard = lax.axis_index("shard")
    core = lax.rem(shard, 2)
    chip = shard // 2
    chips = shards // 2
    sibling = (lang, chip * 2 + 1 - core)
    rows = memory.shape[0]
    width = memory.shape[1]
    cols = width // CHUNKS
    head_cols = key_weight.shape[1]
    block = slots * rows

    loads = [
        pltpu.make_async_copy(key_weight, weights.at[:, 0:head_cols], weight_sem.at[0]),
        pltpu.make_async_copy(
            value_weight, weights.at[:, head_cols : 2 * head_cols], weight_sem.at[1]
        ),
    ]
    for load in loads:
        load.start()
    enter(lang, shard, langs, shards)

    sent = []
    fact_copies = []
    for d in range(1, langs):
        copy = remote(
            facts_in, facts.at[lang], fact_send.at[d], fact_recv.at[d],
            (lax.rem(lang + d, langs), shard),
        )
        copy.start()
        fact_copies.append(copy)
    z_copies = []
    for c in range(CHUNKS):
        part = []
        for d in range(1, langs):
            copy = remote(
                memory.at[:, c * cols : (c + 1) * cols],
                column.at[lang, :, c * cols : (c + 1) * cols],
                z_send.at[d, c], z_recv.at[d, c],
                (lax.rem(lang + d, langs), shard),
            )
            copy.start()
            part.append(copy)
        z_copies.append(part)
    facts[lang] = facts_in[...]
    column[lang] = memory[...]
    for copy in fact_copies:
        copy.wait_recv()
    sent += fact_copies
    chosen = selection(facts, lang, langs, slots)
    for r in range(slots):
        for row, first in ((1, 0), (2, slots)):
            value = jnp.zeros((1, 1), jnp.int32)
            for j in range(langs):
                value = value + chosen[r][j] * facts[j, row : row + 1, 0:1]
            lengths[first + r : first + r + 1, :] = jnp.broadcast_to(value, (1, 128))
    weigh = [[chosen[r][j].astype(F32) for j in range(langs)] for r in range(slots)]

    def window(who, c):
        return group.at[pl.ds(pl.multiple_of(who * block, block), block), c * cols : (c + 1) * cols]

    p_copies = []
    s_copies = []
    for c in range(CHUNKS):
        for copy in z_copies[c]:
            copy.wait_recv()
        sent += z_copies[c]
        for r in range(slots):
            value = jnp.zeros((rows, cols), F32)
            for j in range(langs):
                value = value + column[j, :, c * cols : (c + 1) * cols].astype(F32) * weigh[r][j]
            start = pl.multiple_of(shard * block + r * rows, rows)
            group[pl.ds(start, rows), c * cols : (c + 1) * cols] = value.astype(BF16)
        part = []
        for d in range(1, chips):
            target = lax.rem(chip + d, chips) * 2 + core
            copy = remote(
                window(shard, c), window(shard, c), p_send.at[d, c], p_recv.at[d, c],
                (lang, target),
            )
            copy.start()
            part.append(copy)
        p_copies.append(part)
        copy = remote(window(shard, c), window(shard, c), s_send.at[0, c], s_recv.at[0, c], sibling)
        copy.start()
        s_copies.append([copy])
    for load in loads:
        load.wait()
    for c in range(CHUNKS):
        for d in range(1, chips):
            p_copies[c][d - 1].wait_recv()
            source = lax.rem(chip + chips - d, chips) * 2 + core
            copy = remote(
                window(source, c), window(source, c), s_send.at[d, c], s_recv.at[d, c], sibling
            )
            copy.start()
            s_copies[c].append(copy)
        sent += p_copies[c]
        for copy in s_copies[c]:
            copy.wait_recv()
        sent += s_copies[c]
        product = jnp.dot(
            group[:, c * cols : (c + 1) * cols],
            weights[c * cols : (c + 1) * cols, :],
            preferred_element_type=F32,
        )
        if c == 0:
            total[...] = product
        elif c < CHUNKS - 1:
            total[...] += product
        else:
            product = total[...] + product
            outgoing[...] = product.astype(BF16).reshape(outgoing.shape)
    exchange(lang, shard, shards, outgoing, rows_out, a_send, a_recv)
    for copy in sent:
        copy.wait_send()


def exchange(lang, shard, shards, outgoing, incoming, send_sem, recv_sem):
    copies = []
    for d in range(1, shards):
        target = lax.rem(shard + d, shards)
        copy = remote(
            outgoing.at[target], incoming.at[shard], send_sem.at[d], recv_sem.at[d], (lang, target)
        )
        copy.start()
        copies.append(copy)
    incoming[shard] = outgoing[shard]
    for copy in copies:
        copy.wait_recv()
    for copy in copies:
        copy.wait_send()


def attend_kernel(lengths, queries, grads, rows_in, context, grad_queries, grad_rows):
    slot = pl.program_id(0)
    groups = rows_in.shape[0]
    source_rows = rows_in.shape[1]
    head_cols = rows_in.shape[2] // 2
    target_rows = queries.shape[2]
    heads = head_cols // HEAD
    span = heads * source_rows
    scaling = HEAD ** (-0.5)
    slots = pl.num_programs(0)
    src = lengths[pl.ds(slot, 1), :]
    tgt = lengths[pl.ds(slots + slot, 1), :]
    src = jnp.maximum(src, 1)[:, 0:1].reshape(1, 1, 1)
    tgt = tgt[:, 0:1]
    key_valid = lax.broadcasted_iota(jnp.int32, (heads, source_rows, target_rows), 1) < src
    row_keep = lax.broadcasted_iota(jnp.int32, (target_rows, head_cols), 0) < tgt
    same = (
        lax.broadcasted_iota(jnp.int32, (span, head_cols), 0) // source_rows
        == lax.broadcasted_iota(jnp.int32, (span, head_cols), 1) // HEAD
    )

    def spread(rows):
        wide = jnp.concatenate([rows] * heads, axis=0) if heads > 1 else rows
        return jnp.where(same, wide.astype(F32), 0.0).astype(BF16)

    def gather(wide):
        return jnp.concatenate(
            [
                wide[h * source_rows : (h + 1) * source_rows, h * HEAD : (h + 1) * HEAD]
                for h in range(heads)
            ],
            axis=1,
        )

    nt = (((1,), (1,)), ((), ()))
    tn = (((0,), (0,)), ((), ()))
    for g in range(groups):
        lanes = slice(g * head_cols, (g + 1) * head_cols)
        q = queries[0, 0, :, lanes]
        grad = jnp.where(row_keep, grads[0, 0, :, lanes].astype(F32), 0.0).astype(BF16)
        keys = spread(rows_in[g, :, :head_cols])
        values = spread(rows_in[g, :, head_cols:])
        scores = lax.dot_general(keys, q, nt, preferred_element_type=F32) * scaling
        scores = scores.reshape(heads, source_rows, target_rows)
        scores = jnp.where(key_valid, scores, masked_score)
        shifted = jnp.exp(scores - jnp.max(scores, axis=1, keepdims=True))
        attention = shifted / jnp.sum(shifted, axis=1, keepdims=True)
        attention_bf = attention.reshape(span, target_rows).astype(BF16)
        out = lax.dot_general(attention_bf, values, tn, preferred_element_type=F32)
        context[0, 0, :, lanes] = jnp.where(row_keep, out, 0.0).astype(BF16)
        grad_values = jnp.dot(attention_bf, grad, preferred_element_type=F32)
        grad_attention = lax.dot_general(values, grad, nt, preferred_element_type=F32)
        grad_attention = grad_attention.reshape(heads, source_rows, target_rows)
        row_dot = jnp.sum(attention * grad_attention, axis=1, keepdims=True)
        grad_scores = attention * (grad_attention - row_dot)
        grad_scores = grad_scores.reshape(span, target_rows).astype(BF16)
        out = lax.dot_general(grad_scores, keys, tn, preferred_element_type=F32)
        grad_queries[0, 0, :, lanes] = (out * scaling).astype(BF16)
        grad_keys = jnp.dot(grad_scores, q, preferred_element_type=F32) * scaling
        grad_rows[g, :, :head_cols] = gather(grad_keys).astype(BF16)
        grad_rows[g, :, head_cols:] = gather(grad_values).astype(BF16)


def reduce_kernel(
    langs, shards, slots,
    grad_rows, facts, key_weight, value_weight,
    grad_memory, all_rows,
    weights, partial, first, paired, second, returning, third,
    weight_sem, a_send, a_recv, f_send, f_recv, p_send, p_recv, z_send, z_recv,
):
    lang = lax.axis_index("lang")
    shard = lax.axis_index("shard")
    core = lax.rem(shard, 2)
    chip = shard // 2
    chips = shards // 2
    sibling = (lang, chip * 2 + 1 - core)
    rows = grad_memory.shape[0]
    cols = grad_memory.shape[1] // CHUNKS
    head_cols = key_weight.shape[1]
    block = slots * rows
    nt = (((1,), (1,)), ((), ()))

    loads = [
        pltpu.make_async_copy(key_weight, weights.at[:, 0:head_cols], weight_sem.at[0]),
        pltpu.make_async_copy(
            value_weight, weights.at[:, head_cols : 2 * head_cols], weight_sem.at[1]
        ),
    ]
    for load in loads:
        load.start()
    enter(lang, shard, langs, shards)
    exchange(lang, shard, shards, grad_rows, all_rows, a_send, a_recv)
    for load in loads:
        load.wait()

    sent = []
    f_copies = []
    for c in range(CHUNKS):
        product = lax.dot_general(
            all_rows[...].reshape(shards * block, 2 * head_cols),
            weights[c * cols : (c + 1) * cols, :],
            nt,
            preferred_element_type=F32,
        )
        product = product.astype(BF16).reshape(chips, 2, block, cols)
        partial[c, 0] = product[:, 0]
        partial[c, 1] = product[:, 1]
        copy = remote(
            partial.at[c, 1 - core], first.at[c], f_send.at[c], f_recv.at[c], sibling
        )
        copy.start()
        f_copies.append(copy)
    p_copies = []
    for c in range(CHUNKS):
        f_copies[c].wait_recv()
        part = []
        for d in range(1, chips):
            other = lax.rem(chip + d, chips)
            pair = partial[c, core, other].astype(F32) + first[c, other].astype(F32)
            paired[c, d] = pair.astype(BF16)
            copy = remote(
                paired.at[c, d], second.at[c, d], p_send.at[c, d], p_recv.at[c, d],
                (lang, other * 2 + core),
            )
            copy.start()
            part.append(copy)
        p_copies.append(part)
    sent += f_copies
    chosen = selection(facts, lang, langs, slots)
    weigh = [[chosen[r][j].astype(F32) for j in range(langs)] for r in range(slots)]
    z_copies = []
    for c in range(CHUNKS):
        value = partial[c, core, chip].astype(F32) + first[c, chip].astype(F32)
        for d in range(1, chips):
            p_copies[c][d - 1].wait_recv()
            value = value + second[c, d].astype(F32)
        sent += p_copies[c]
        value = value.astype(BF16).astype(F32)
        for j in range(langs):
            back = value[0:rows] * weigh[0][j]
            for r in range(1, slots):
                back = back + value[r * rows : (r + 1) * rows] * weigh[r][j]
            returning[c, j] = back.astype(BF16)
        part = []
        for d in range(1, langs):
            other = lax.rem(lang + d, langs)
            copy = remote(
                returning.at[c, other], third.at[c, d], z_send.at[c, d], z_recv.at[c, d],
                (other, shard),
            )
            copy.start()
            part.append(copy)
        z_copies.append(part)
    for c in range(CHUNKS):
        value = returning[c, lang].astype(F32)
        for d in range(1, langs):
            z_copies[c][d - 1].wait_recv()
            value = value + third[c, d].astype(F32)
        sent += z_copies[c]
        grad_memory[:, c * cols : (c + 1) * cols] = value.astype(BF16)
    for copy in sent:
        copy.wait_send()


def local(memory, lang_id, src_len, tgt_len, queries, key_weight, value_weight, grad_context):
    langs = lax.axis_size("lang")
    shards = lax.axis_size("shard")
    chips = shards // 2
    slots = queries.shape[1]
    target_rows = queries.shape[2]
    rows = memory.shape[1]
    width = memory.shape[2]
    head_cols = key_weight.shape[2]
    cols = width // CHUNKS
    block = slots * rows
    total_rows = shards * block
    vmem = pl.BlockSpec(memory_space=pltpu.VMEM)
    hbm = pl.BlockSpec(memory_space=pl.ANY)
    dma = pltpu.SemaphoreType.DMA
    keys = key_weight[0]
    values = value_weight[0]
    facts_in = jnp.concatenate([lang_id, src_len, tgt_len, jnp.zeros((5,), jnp.int32)])
    facts_in = jnp.broadcast_to(facts_in[:, None], (8, 128))

    group, rows_in, facts, lengths = pl.pallas_call(
        functools.partial(route_kernel, langs, shards, slots),
        out_shape=(
            jax.ShapeDtypeStruct((total_rows, width), BF16),
            jax.ShapeDtypeStruct((shards, block, 2 * head_cols), BF16),
            jax.ShapeDtypeStruct((langs, 8, 128), jnp.int32),
            jax.ShapeDtypeStruct((2 * slots, 128), jnp.int32),
        ),
        in_specs=[vmem, vmem, hbm, hbm],
        out_specs=(vmem, vmem, vmem, vmem),
        scratch_shapes=[
            pltpu.VMEM((langs, rows, width), BF16),
            pltpu.VMEM((width, 2 * head_cols), BF16),
            pltpu.VMEM((total_rows, 2 * head_cols), F32),
            pltpu.VMEM((shards, block, 2 * head_cols), BF16),
            dma((2,)),
            dma((langs,)),
            dma((langs,)),
            dma((langs, CHUNKS)),
            dma((langs, CHUNKS)),
            dma((chips, CHUNKS)),
            dma((chips, CHUNKS)),
            dma((chips, CHUNKS)),
            dma((chips, CHUNKS)),
            dma((shards,)),
            dma((shards,)),
        ],
        compiler_params=pltpu.CompilerParams(
            collective_id=0, has_side_effects=True, vmem_limit_bytes=VMEM_BYTES
        ),
        name="route_and_project",
    )(memory[0], facts_in, keys, values)

    per_step = max(1, min(shards, 1024 // head_cols))
    steps = shards // per_step
    wide = pl.BlockSpec(
        (1, 1, target_rows, per_step * head_cols), lambda r, p: (0, r, 0, p)
    )
    narrow = pl.BlockSpec((per_step, rows, 2 * head_cols), lambda r, p: (p, r, 0))
    context, grad_queries, grad_rows = pl.pallas_call(
        attend_kernel,
        grid=(slots, steps),
        out_shape=(
            jax.ShapeDtypeStruct(queries.shape, BF16),
            jax.ShapeDtypeStruct(queries.shape, BF16),
            jax.ShapeDtypeStruct(rows_in.shape, BF16),
        ),
        in_specs=[
            pl.BlockSpec((2 * slots, 128), lambda r, p: (0, 0)), wide, wide, narrow
        ],
        out_specs=(wide, wide, narrow),
        compiler_params=pltpu.CompilerParams(vmem_limit_bytes=VMEM_BYTES),
        name="attend_both_ways",
    )(lengths, queries, grad_context, rows_in)

    grad_memory, all_rows = pl.pallas_call(
        functools.partial(reduce_kernel, langs, shards, slots),
        out_shape=(
            jax.ShapeDtypeStruct((rows, width), BF16),
            jax.ShapeDtypeStruct((shards, block, 2 * head_cols), BF16),
        ),
        in_specs=[vmem, vmem, hbm, hbm],
        out_specs=(vmem, vmem),
        scratch_shapes=[
            pltpu.VMEM((width, 2 * head_cols), BF16),
            pltpu.VMEM((CHUNKS, 2, chips, block, cols), BF16),
            pltpu.VMEM((CHUNKS, chips, block, cols), BF16),
            pltpu.VMEM((CHUNKS, chips, block, cols), BF16),
            pltpu.VMEM((CHUNKS, chips, block, cols), BF16),
            pltpu.VMEM((CHUNKS, langs, rows, cols), BF16),
            pltpu.VMEM((CHUNKS, langs, rows, cols), BF16),
            dma((2,)),
            dma((shards,)),
            dma((shards,)),
            dma((CHUNKS,)),
            dma((CHUNKS,)),
            dma((CHUNKS, chips)),
            dma((CHUNKS, chips)),
            dma((CHUNKS, langs)),
            dma((CHUNKS, langs)),
        ],
        compiler_params=pltpu.CompilerParams(
            collective_id=1, has_side_effects=True, vmem_limit_bytes=VMEM_BYTES
        ),
        name="reduce_and_return",
    )(grad_rows, facts, keys, values)

    flat = all_rows.reshape(total_rows, 2 * head_cols)
    tn = (((0,), (0,)), ((), ()))
    grad_key = lax.dot_general(group, flat[:, :head_cols], tn, preferred_element_type=F32)
    grad_value = lax.dot_general(group, flat[:, head_cols:], tn, preferred_element_type=F32)
    return (
        context,
        grad_queries,
        grad_memory[None],
        grad_key.astype(BF16)[None],
        grad_value.astype(BF16)[None],
    )


def solution(mesh):
    return jax.shard_map(
        local,
        mesh=mesh,
        in_specs=(
            P(("lang", "shard"), None, None),
            P(("lang", "shard")),
            P(("lang", "shard")),
            P(("lang", "shard")),
            P("lang", "shard", None, None),
            P("lang", None, "shard"),
            P("lang", None, "shard"),
            P("lang", "shard", None, None),
        ),
        out_specs=(
            P("lang", "shard", None, None),
            P("lang", "shard", None, None),
            P(("lang", "shard"), None, None),
            P("lang", None, "shard"),
            P("lang", None, "shard"),
        ),
        check_vma=False,
    )
```

```python
import functools

import jax
import jax.numpy as jnp
from jax import lax
from jax.experimental import pallas as pl
from jax.experimental.pallas import tpu as pltpu
from jax.sharding import PartitionSpec as P

HEAD = 128
CHUNKS = 4
AHEAD = 2
VMEM_BYTES = 50 * 1024 * 1024

masked_score = -1e30
MESH = pl.DeviceIdType.MESH
F32 = jnp.float32
BF16 = jnp.bfloat16


def remote(src, dst, send_sem, recv_sem, device):
    return pltpu.make_async_remote_copy(
        src_ref=src,
        dst_ref=dst,
        send_sem=send_sem,
        recv_sem=recv_sem,
        device_id=device,
        device_id_type=MESH,
    )


def enter(lang, shard, langs, shards):
    barrier = pltpu.get_barrier_semaphore()
    for step in range(1, langs):
        pl.semaphore_signal(
            barrier, inc=1, device_id=(lax.rem(lang + step, langs), shard), device_id_type=MESH
        )
    for step in range(1, shards):
        pl.semaphore_signal(
            barrier, inc=1, device_id=(lang, lax.rem(shard + step, shards)), device_id_type=MESH
        )
    pl.semaphore_wait(barrier, langs + shards - 2)


def selection(facts, lang, langs, slots):
    ids = [facts[j, 0:1, 0:1] for j in range(langs)]
    chosen = [[None] * langs for _ in range(slots)]
    for j in range(langs):
        rank = jnp.zeros((1, 1), jnp.int32)
        for k in range(j):
            rank = rank + jnp.where(ids[k] == ids[j], 1, 0)
        here = ids[j] == lang
        for r in range(slots):
            chosen[r][j] = jnp.where(here & (rank == r), 1, 0)
    return chosen


def route_kernel(
    langs, shards, slots,
    memory, facts_in, key_weight, value_weight,
    group, rows_out, facts, lengths,
    column, weights, total, outgoing,
    weight_sem, fact_send, fact_recv, z_send, z_recv,
    p_send, p_recv, s_send, s_recv, a_send, a_recv,
):
    lang = lax.axis_index("lang")
    shard = lax.axis_index("shard")
    core = lax.rem(shard, 2)
    chip = shard // 2
    chips = shards // 2
    sibling = (lang, chip * 2 + 1 - core)
    rows = memory.shape[0]
    width = memory.shape[1]
    cols = width // CHUNKS
    head_cols = key_weight.shape[1]
    block = slots * rows

    loads = [
        pltpu.make_async_copy(key_weight, weights.at[:, 0:head_cols], weight_sem.at[0]),
        pltpu.make_async_copy(
            value_weight, weights.at[:, head_cols : 2 * head_cols], weight_sem.at[1]
        ),
    ]
    for load in loads:
        load.start()
    enter(lang, shard, langs, shards)

    sent = []
    fact_copies = []
    for d in range(1, langs):
        copy = remote(
            facts_in, facts.at[lang], fact_send.at[d], fact_recv.at[d],
            (lax.rem(lang + d, langs), shard),
        )
        copy.start()
        fact_copies.append(copy)
    z_copies = []

    def start_z(c):
        part = []
        for d in range(1, langs):
            copy = remote(
                memory.at[:, c * cols : (c + 1) * cols],
                column.at[lang, :, c * cols : (c + 1) * cols],
                z_send.at[d, c], z_recv.at[d, c],
                (lax.rem(lang + d, langs), shard),
            )
            copy.start()
            part.append(copy)
        z_copies.append(part)

    for c in range(min(AHEAD, CHUNKS)):
        start_z(c)
    facts[lang] = facts_in[...]
    column[lang] = memory[...]
    for copy in fact_copies:
        copy.wait_recv()
    sent += fact_copies
    chosen = selection(facts, lang, langs, slots)
    for r in range(slots):
        for row, first in ((1, 0), (2, slots)):
            value = jnp.zeros((1, 1), jnp.int32)
            for j in range(langs):
                value = value + chosen[r][j] * facts[j, row : row + 1, 0:1]
            lengths[first + r : first + r + 1, :] = jnp.broadcast_to(value, (1, 128))
    weigh = [[chosen[r][j].astype(F32) for j in range(langs)] for r in range(slots)]

    def window(who, c):
        return group.at[pl.ds(pl.multiple_of(who * block, block), block), c * cols : (c + 1) * cols]

    p_copies = []
    s_copies = []

    def route(c):
        for copy in z_copies[c]:
            copy.wait_recv()
        sent.extend(z_copies[c])
        if c + AHEAD < CHUNKS:
            start_z(c + AHEAD)
        for r in range(slots):
            value = jnp.zeros((rows, cols), F32)
            for j in range(langs):
                value = value + column[j, :, c * cols : (c + 1) * cols].astype(F32) * weigh[r][j]
            start = pl.multiple_of(shard * block + r * rows, rows)
            group[pl.ds(start, rows), c * cols : (c + 1) * cols] = value.astype(BF16)
        part = []
        for d in range(1, chips):
            target = lax.rem(chip + d, chips) * 2 + core
            copy = remote(
                window(shard, c), window(shard, c), p_send.at[d, c], p_recv.at[d, c],
                (lang, target),
            )
            copy.start()
            part.append(copy)
        p_copies.append(part)
        copy = remote(window(shard, c), window(shard, c), s_send.at[0, c], s_recv.at[0, c], sibling)
        copy.start()
        s_copies.append([copy])

    def forward(c):
        for d in range(1, chips):
            p_copies[c][d - 1].wait_recv()
            source = lax.rem(chip + chips - d, chips) * 2 + core
            copy = remote(
                window(source, c), window(source, c), s_send.at[d, c], s_recv.at[d, c], sibling
            )
            copy.start()
            s_copies[c].append(copy)
        sent.extend(p_copies[c])

    def project(c):
        for copy in s_copies[c]:
            copy.wait_recv()
        sent.extend(s_copies[c])
        product = jnp.dot(
            group[:, c * cols : (c + 1) * cols],
            weights[c * cols : (c + 1) * cols, :],
            preferred_element_type=F32,
        )
        if c == 0:
            total[...] = product
        elif c < CHUNKS - 1:
            total[...] += product
        else:
            product = total[...] + product
            outgoing[...] = product.astype(BF16).reshape(outgoing.shape)

    for turn in range(CHUNKS + 2):
        if turn < CHUNKS:
            route(turn)
        if 0 <= turn - 1 < CHUNKS:
            forward(turn - 1)
        if turn == 2:
            for load in loads:
                load.wait()
        if 0 <= turn - 2:
            project(turn - 2)
    exchange(lang, shard, shards, outgoing, rows_out, a_send, a_recv)
    for copy in sent:
        copy.wait_send()


def exchange(lang, shard, shards, outgoing, incoming, send_sem, recv_sem):
    copies = []
    for d in range(1, shards):
        target = lax.rem(shard + d, shards)
        copy = remote(
            outgoing.at[target], incoming.at[shard], send_sem.at[d], recv_sem.at[d], (lang, target)
        )
        copy.start()
        copies.append(copy)
    incoming[shard] = outgoing[shard]
    for copy in copies:
        copy.wait_recv()
    for copy in copies:
        copy.wait_send()


def attend_kernel(lengths, queries, grads, rows_in, context, grad_queries, grad_rows):
    slot = pl.program_id(0)
    groups = rows_in.shape[0]
    source_rows = rows_in.shape[1]
    head_cols = rows_in.shape[2] // 2
    target_rows = queries.shape[2]
    heads = head_cols // HEAD
    span = heads * source_rows
    scaling = HEAD ** (-0.5)
    slots = pl.num_programs(0)
    src = lengths[pl.ds(slot, 1), :]
    tgt = lengths[pl.ds(slots + slot, 1), :]
    src = jnp.maximum(src, 1)[:, 0:1].reshape(1, 1, 1)
    tgt = tgt[:, 0:1]
    key_valid = lax.broadcasted_iota(jnp.int32, (heads, source_rows, target_rows), 1) < src
    row_keep = lax.broadcasted_iota(jnp.int32, (target_rows, head_cols), 0) < tgt
    same = (
        lax.broadcasted_iota(jnp.int32, (span, head_cols), 0) // source_rows
        == lax.broadcasted_iota(jnp.int32, (span, head_cols), 1) // HEAD
    )

    def spread(rows):
        wide = jnp.concatenate([rows] * heads, axis=0) if heads > 1 else rows
        return jnp.where(same, wide.astype(F32), 0.0).astype(BF16)

    def gather(wide):
        return jnp.concatenate(
            [
                wide[h * source_rows : (h + 1) * source_rows, h * HEAD : (h + 1) * HEAD]
                for h in range(heads)
            ],
            axis=1,
        )

    nt = (((1,), (1,)), ((), ()))
    tn = (((0,), (0,)), ((), ()))
    for g in range(groups):
        lanes = slice(g * head_cols, (g + 1) * head_cols)
        q = queries[0, 0, :, lanes]
        grad = jnp.where(row_keep, grads[0, 0, :, lanes].astype(F32), 0.0).astype(BF16)
        keys = spread(rows_in[g, :, :head_cols])
        values = spread(rows_in[g, :, head_cols:])
        scores = lax.dot_general(keys, q, nt, preferred_element_type=F32) * scaling
        scores = scores.reshape(heads, source_rows, target_rows)
        scores = jnp.where(key_valid, scores, masked_score)
        shifted = jnp.exp(scores - jnp.max(scores, axis=1, keepdims=True))
        attention = shifted / jnp.sum(shifted, axis=1, keepdims=True)
        attention_bf = attention.reshape(span, target_rows).astype(BF16)
        out = lax.dot_general(attention_bf, values, tn, preferred_element_type=F32)
        context[0, 0, :, lanes] = jnp.where(row_keep, out, 0.0).astype(BF16)
        grad_values = jnp.dot(attention_bf, grad, preferred_element_type=F32)
        grad_attention = lax.dot_general(values, grad, nt, preferred_element_type=F32)
        grad_attention = grad_attention.reshape(heads, source_rows, target_rows)
        row_dot = jnp.sum(attention * grad_attention, axis=1, keepdims=True)
        grad_scores = attention * (grad_attention - row_dot)
        grad_scores = grad_scores.reshape(span, target_rows).astype(BF16)
        out = lax.dot_general(grad_scores, keys, tn, preferred_element_type=F32)
        grad_queries[0, 0, :, lanes] = (out * scaling).astype(BF16)
        grad_keys = jnp.dot(grad_scores, q, preferred_element_type=F32) * scaling
        grad_rows[g, :, :head_cols] = gather(grad_keys).astype(BF16)
        grad_rows[g, :, head_cols:] = gather(grad_values).astype(BF16)


def reduce_kernel(
    langs, shards, slots,
    grad_rows, facts, key_weight, value_weight,
    grad_memory, all_rows,
    weights, partial, first, paired, second, returning, third,
    weight_sem, a_send, a_recv, f_send, f_recv, p_send, p_recv, z_send, z_recv,
):
    lang = lax.axis_index("lang")
    shard = lax.axis_index("shard")
    core = lax.rem(shard, 2)
    chip = shard // 2
    chips = shards // 2
    sibling = (lang, chip * 2 + 1 - core)
    rows = grad_memory.shape[0]
    cols = grad_memory.shape[1] // CHUNKS
    head_cols = key_weight.shape[1]
    block = slots * rows
    nt = (((1,), (1,)), ((), ()))

    loads = [
        pltpu.make_async_copy(key_weight, weights.at[:, 0:head_cols], weight_sem.at[0]),
        pltpu.make_async_copy(
            value_weight, weights.at[:, head_cols : 2 * head_cols], weight_sem.at[1]
        ),
    ]
    for load in loads:
        load.start()
    enter(lang, shard, langs, shards)
    exchange(lang, shard, shards, grad_rows, all_rows, a_send, a_recv)
    for load in loads:
        load.wait()

    sent = []
    f_copies = []
    for c in range(CHUNKS):
        product = lax.dot_general(
            all_rows[...].reshape(shards * block, 2 * head_cols),
            weights[c * cols : (c + 1) * cols, :],
            nt,
            preferred_element_type=F32,
        )
        product = product.astype(BF16).reshape(chips, 2, block, cols)
        partial[c, 0] = product[:, 0]
        partial[c, 1] = product[:, 1]
        copy = remote(
            partial.at[c, 1 - core], first.at[c], f_send.at[c], f_recv.at[c], sibling
        )
        copy.start()
        f_copies.append(copy)
        if c == min(1, CHUNKS - 1):
            chosen = selection(facts, lang, langs, slots)
            weigh = [[chosen[r][j].astype(F32) for j in range(langs)] for r in range(slots)]
    p_copies = []
    z_copies = []

    def send_pairs(c):
        f_copies[c].wait_recv()
        part = []
        for d in range(1, chips):
            other = lax.rem(chip + d, chips)
            pair = partial[c, core, other].astype(F32) + first[c, other].astype(F32)
            paired[c, d] = pair.astype(BF16)
            copy = remote(
                paired.at[c, d], second.at[c, d], p_send.at[c, d], p_recv.at[c, d],
                (lang, other * 2 + core),
            )
            copy.start()
            part.append(copy)
        p_copies.append(part)

    def send_back(c):
        value = partial[c, core, chip].astype(F32) + first[c, chip].astype(F32)
        for d in range(1, chips):
            p_copies[c][d - 1].wait_recv()
            value = value + second[c, d].astype(F32)
        value = value.astype(BF16).astype(F32)
        for j in range(langs):
            back = value[0:rows] * weigh[0][j]
            for r in range(1, slots):
                back = back + value[r * rows : (r + 1) * rows] * weigh[r][j]
            returning[c, j] = back.astype(BF16)
        part = []
        for d in range(1, langs):
            other = lax.rem(lang + d, langs)
            copy = remote(
                returning.at[c, other], third.at[c, d], z_send.at[c, d], z_recv.at[c, d],
                (other, shard),
            )
            copy.start()
            part.append(copy)
        z_copies.append(part)

    def finish(c):
        value = returning[c, lang].astype(F32)
        for d in range(1, langs):
            z_copies[c][d - 1].wait_recv()
            value = value + third[c, d].astype(F32)
        grad_memory[:, c * cols : (c + 1) * cols] = value.astype(BF16)

    for turn in range(CHUNKS + 1):
        if turn < CHUNKS:
            send_pairs(turn)
        if 0 <= turn - 1:
            send_back(turn - 1)
    for c in range(CHUNKS):
        finish(c)
    sent += f_copies
    for c in range(CHUNKS):
        sent += p_copies[c] + z_copies[c]
    for copy in sent:
        copy.wait_send()


def local(memory, lang_id, src_len, tgt_len, queries, key_weight, value_weight, grad_context):
    langs = lax.axis_size("lang")
    shards = lax.axis_size("shard")
    chips = shards // 2
    slots = queries.shape[1]
    target_rows = queries.shape[2]
    rows = memory.shape[1]
    width = memory.shape[2]
    head_cols = key_weight.shape[2]
    cols = width // CHUNKS
    block = slots * rows
    total_rows = shards * block
    vmem = pl.BlockSpec(memory_space=pltpu.VMEM)
    hbm = pl.BlockSpec(memory_space=pl.ANY)
    dma = pltpu.SemaphoreType.DMA
    keys = key_weight[0]
    values = value_weight[0]
    facts_in = jnp.concatenate([lang_id, src_len, tgt_len, jnp.zeros((5,), jnp.int32)])
    facts_in = jnp.broadcast_to(facts_in[:, None], (8, 128))

    group, rows_in, facts, lengths = pl.pallas_call(
        functools.partial(route_kernel, langs, shards, slots),
        out_shape=(
            jax.ShapeDtypeStruct((total_rows, width), BF16),
            jax.ShapeDtypeStruct((shards, block, 2 * head_cols), BF16),
            jax.ShapeDtypeStruct((langs, 8, 128), jnp.int32),
            jax.ShapeDtypeStruct((2 * slots, 128), jnp.int32),
        ),
        in_specs=[vmem, vmem, hbm, hbm],
        out_specs=(vmem, vmem, vmem, vmem),
        scratch_shapes=[
            pltpu.VMEM((langs, rows, width), BF16),
            pltpu.VMEM((width, 2 * head_cols), BF16),
            pltpu.VMEM((total_rows, 2 * head_cols), F32),
            pltpu.VMEM((shards, block, 2 * head_cols), BF16),
            dma((2,)),
            dma((langs,)),
            dma((langs,)),
            dma((langs, CHUNKS)),
            dma((langs, CHUNKS)),
            dma((chips, CHUNKS)),
            dma((chips, CHUNKS)),
            dma((chips, CHUNKS)),
            dma((chips, CHUNKS)),
            dma((shards,)),
            dma((shards,)),
        ],
        compiler_params=pltpu.CompilerParams(
            collective_id=0, has_side_effects=True, vmem_limit_bytes=VMEM_BYTES
        ),
        name="route_and_project",
    )(memory[0], facts_in, keys, values)

    per_step = max(1, min(shards, 1024 // head_cols))
    steps = shards // per_step
    wide = pl.BlockSpec(
        (1, 1, target_rows, per_step * head_cols), lambda r, p: (0, r, 0, p)
    )
    narrow = pl.BlockSpec((per_step, rows, 2 * head_cols), lambda r, p: (p, r, 0))
    context, grad_queries, grad_rows = pl.pallas_call(
        attend_kernel,
        grid=(slots, steps),
        out_shape=(
            jax.ShapeDtypeStruct(queries.shape, BF16),
            jax.ShapeDtypeStruct(queries.shape, BF16),
            jax.ShapeDtypeStruct(rows_in.shape, BF16),
        ),
        in_specs=[
            pl.BlockSpec((2 * slots, 128), lambda r, p: (0, 0)), wide, wide, narrow
        ],
        out_specs=(wide, wide, narrow),
        compiler_params=pltpu.CompilerParams(vmem_limit_bytes=VMEM_BYTES),
        name="attend_both_ways",
    )(lengths, queries, grad_context, rows_in)

    grad_memory, all_rows = pl.pallas_call(
        functools.partial(reduce_kernel, langs, shards, slots),
        out_shape=(
            jax.ShapeDtypeStruct((rows, width), BF16),
            jax.ShapeDtypeStruct((shards, block, 2 * head_cols), BF16),
        ),
        in_specs=[vmem, vmem, hbm, hbm],
        out_specs=(vmem, vmem),
        scratch_shapes=[
            pltpu.VMEM((width, 2 * head_cols), BF16),
            pltpu.VMEM((CHUNKS, 2, chips, block, cols), BF16),
            pltpu.VMEM((CHUNKS, chips, block, cols), BF16),
            pltpu.VMEM((CHUNKS, chips, block, cols), BF16),
            pltpu.VMEM((CHUNKS, chips, block, cols), BF16),
            pltpu.VMEM((CHUNKS, langs, rows, cols), BF16),
            pltpu.VMEM((CHUNKS, langs, rows, cols), BF16),
            dma((2,)),
            dma((shards,)),
            dma((shards,)),
            dma((CHUNKS,)),
            dma((CHUNKS,)),
            dma((CHUNKS, chips)),
            dma((CHUNKS, chips)),
            dma((CHUNKS, langs)),
            dma((CHUNKS, langs)),
        ],
        compiler_params=pltpu.CompilerParams(
            collective_id=1, has_side_effects=True, vmem_limit_bytes=VMEM_BYTES
        ),
        name="reduce_and_return",
    )(grad_rows, facts, keys, values)

    flat = all_rows.reshape(total_rows, 2 * head_cols)
    tn = (((0,), (0,)), ((), ()))
    grad_key = lax.dot_general(group, flat[:, :head_cols], tn, preferred_element_type=F32)
    grad_value = lax.dot_general(group, flat[:, head_cols:], tn, preferred_element_type=F32)
    return (
        context,
        grad_queries,
        grad_memory[None],
        grad_key.astype(BF16)[None],
        grad_value.astype(BF16)[None],
    )


def solution(mesh):
    return jax.shard_map(
        local,
        mesh=mesh,
        in_specs=(
            P(("lang", "shard"), None, None),
            P(("lang", "shard")),
            P(("lang", "shard")),
            P(("lang", "shard")),
            P("lang", "shard", None, None),
            P("lang", None, "shard"),
            P("lang", None, "shard"),
            P("lang", "shard", None, None),
        ),
        out_specs=(
            P("lang", "shard", None, None),
            P("lang", "shard", None, None),
            P(("lang", "shard"), None, None),
            P("lang", None, "shard"),
            P("lang", None, "shard"),
        ),
        check_vma=False,
    )
```

```python
import functools

import jax
import jax.numpy as jnp
from jax import lax
from jax.experimental import pallas as pl
from jax.experimental.pallas import tpu as pltpu
from jax.sharding import PartitionSpec as P

HEAD = 128
CHUNKS = 4
AHEAD = 2
VMEM_BYTES = 50 * 1024 * 1024

masked_score = -1e30
MESH = pl.DeviceIdType.MESH
F32 = jnp.float32
BF16 = jnp.bfloat16


def remote(src, dst, send_sem, recv_sem, device):
    return pltpu.make_async_remote_copy(
        src_ref=src,
        dst_ref=dst,
        send_sem=send_sem,
        recv_sem=recv_sem,
        device_id=device,
        device_id_type=MESH,
    )


def enter(lang, shard, langs, shards):
    barrier = pltpu.get_barrier_semaphore()
    for step in range(1, langs):
        pl.semaphore_signal(
            barrier, inc=1, device_id=(lax.rem(lang + step, langs), shard), device_id_type=MESH
        )
    for step in range(1, shards):
        pl.semaphore_signal(
            barrier, inc=1, device_id=(lang, lax.rem(shard + step, shards)), device_id_type=MESH
        )
    pl.semaphore_wait(barrier, langs + shards - 2)


def selection(facts, lang, langs, slots):
    ids = [facts[j, 0:1, 0:1] for j in range(langs)]
    chosen = [[None] * langs for _ in range(slots)]
    for j in range(langs):
        rank = jnp.zeros((1, 1), jnp.int32)
        for k in range(j):
            rank = rank + jnp.where(ids[k] == ids[j], 1, 0)
        here = ids[j] == lang
        for r in range(slots):
            chosen[r][j] = jnp.where(here & (rank == r), 1, 0)
    return chosen


def route_kernel(
    langs, shards, slots,
    memory, facts_in, key_weight, value_weight,
    group, rows_out, facts, lengths,
    column, weights, total, outgoing,
    weight_sem, fact_send, fact_recv, z_send, z_recv,
    p_send, p_recv, s_send, s_recv, a_send, a_recv,
):
    lang = lax.axis_index("lang")
    shard = lax.axis_index("shard")
    core = lax.rem(shard, 2)
    chip = shard // 2
    chips = shards // 2
    sibling = (lang, chip * 2 + 1 - core)
    rows = memory.shape[0]
    width = memory.shape[1]
    cols = width // CHUNKS
    head_cols = key_weight.shape[1]
    block = slots * rows

    loads = [
        pltpu.make_async_copy(key_weight, weights.at[:, 0:head_cols], weight_sem.at[0]),
        pltpu.make_async_copy(
            value_weight, weights.at[:, head_cols : 2 * head_cols], weight_sem.at[1]
        ),
    ]
    for load in loads:
        load.start()
    enter(lang, shard, langs, shards)

    sent = []
    fact_copies = []
    for d in range(1, langs):
        copy = remote(
            facts_in, facts.at[lang], fact_send.at[d], fact_recv.at[d],
            (lax.rem(lang + d, langs), shard),
        )
        copy.start()
        fact_copies.append(copy)
    z_copies = []

    def start_z(c):
        part = []
        for d in range(1, langs):
            copy = remote(
                memory.at[:, c * cols : (c + 1) * cols],
                column.at[lang, :, c * cols : (c + 1) * cols],
                z_send.at[d, c], z_recv.at[d, c],
                (lax.rem(lang + d, langs), shard),
            )
            copy.start()
            part.append(copy)
        z_copies.append(part)

    for c in range(min(AHEAD, CHUNKS)):
        start_z(c)
    facts[lang] = facts_in[...]
    own = pltpu.make_async_copy(memory, column.at[lang], weight_sem.at[2])
    own.start()
    own.wait()
    for copy in fact_copies:
        copy.wait_recv()
    sent += fact_copies
    chosen = selection(facts, lang, langs, slots)
    for r in range(slots):
        for row, first in ((1, 0), (2, slots)):
            value = jnp.zeros((1, 1), jnp.int32)
            for j in range(langs):
                value = value + chosen[r][j] * facts[j, row : row + 1, 0:1]
            lengths[first + r : first + r + 1, :] = jnp.broadcast_to(value, (1, 128))
    weigh = [[chosen[r][j].astype(F32) for j in range(langs)] for r in range(slots)]

    def window(who, c):
        return group.at[pl.ds(pl.multiple_of(who * block, block), block), c * cols : (c + 1) * cols]

    p_copies = []
    s_copies = []

    def route(c):
        for copy in z_copies[c]:
            copy.wait_recv()
        sent.extend(z_copies[c])
        if c + AHEAD < CHUNKS:
            start_z(c + AHEAD)
        for r in range(slots):
            value = jnp.zeros((rows, cols), F32)
            for j in range(langs):
                value = value + column[j, :, c * cols : (c + 1) * cols].astype(F32) * weigh[r][j]
            start = pl.multiple_of(shard * block + r * rows, rows)
            group[pl.ds(start, rows), c * cols : (c + 1) * cols] = value.astype(BF16)
        part = []
        for d in range(1, chips):
            target = lax.rem(chip + d, chips) * 2 + core
            copy = remote(
                window(shard, c), window(shard, c), p_send.at[d, c], p_recv.at[d, c],
                (lang, target),
            )
            copy.start()
            part.append(copy)
        p_copies.append(part)
        copy = remote(window(shard, c), window(shard, c), s_send.at[0, c], s_recv.at[0, c], sibling)
        copy.start()
        s_copies.append([copy])

    def forward(c):
        for d in range(1, chips):
            p_copies[c][d - 1].wait_recv()
            source = lax.rem(chip + chips - d, chips) * 2 + core
            copy = remote(
                window(source, c), window(source, c), s_send.at[d, c], s_recv.at[d, c], sibling
            )
            copy.start()
            s_copies[c].append(copy)
        sent.extend(p_copies[c])

    def project(c):
        for copy in s_copies[c]:
            copy.wait_recv()
        sent.extend(s_copies[c])
        product = jnp.dot(
            group[:, c * cols : (c + 1) * cols],
            weights[c * cols : (c + 1) * cols, :],
            preferred_element_type=F32,
        )
        if c == 0:
            total[...] = product
        elif c < CHUNKS - 1:
            total[...] += product
        else:
            product = total[...] + product
            outgoing[...] = product.astype(BF16).reshape(outgoing.shape)

    for turn in range(CHUNKS + 2):
        if turn < CHUNKS:
            route(turn)
        if 0 <= turn - 1 < CHUNKS:
            forward(turn - 1)
        if turn == 2:
            for load in loads:
                load.wait()
        if 0 <= turn - 2:
            project(turn - 2)
    exchange(lang, shard, shards, outgoing, rows_out, a_send, a_recv)
    for copy in sent:
        copy.wait_send()


def exchange(lang, shard, shards, outgoing, incoming, send_sem, recv_sem):
    copies = []
    for d in range(1, shards):
        target = lax.rem(shard + d, shards)
        copy = remote(
            outgoing.at[target], incoming.at[shard], send_sem.at[d], recv_sem.at[d], (lang, target)
        )
        copy.start()
        copies.append(copy)
    incoming[shard] = outgoing[shard]
    for copy in copies:
        copy.wait_recv()
    for copy in copies:
        copy.wait_send()


def attend_kernel(lengths, queries, grads, rows_in, context, grad_queries, grad_rows):
    slot = pl.program_id(0)
    groups = rows_in.shape[0]
    source_rows = rows_in.shape[1]
    head_cols = rows_in.shape[2] // 2
    target_rows = queries.shape[2]
    heads = head_cols // HEAD
    span = heads * source_rows
    scaling = HEAD ** (-0.5)
    slots = pl.num_programs(0)
    src = lengths[pl.ds(slot, 1), :]
    tgt = lengths[pl.ds(slots + slot, 1), :]
    src = jnp.maximum(src, 1)[:, 0:1].reshape(1, 1, 1)
    tgt = tgt[:, 0:1]
    key_valid = lax.broadcasted_iota(jnp.int32, (heads, source_rows, target_rows), 1) < src
    row_keep = lax.broadcasted_iota(jnp.int32, (target_rows, head_cols), 0) < tgt
    same = (
        lax.broadcasted_iota(jnp.int32, (span, head_cols), 0) // source_rows
        == lax.broadcasted_iota(jnp.int32, (span, head_cols), 1) // HEAD
    )

    def spread(rows):
        wide = jnp.concatenate([rows] * heads, axis=0) if heads > 1 else rows
        return jnp.where(same, wide.astype(F32), 0.0).astype(BF16)

    def gather(wide):
        return jnp.concatenate(
            [
                wide[h * source_rows : (h + 1) * source_rows, h * HEAD : (h + 1) * HEAD]
                for h in range(heads)
            ],
            axis=1,
        )

    nt = (((1,), (1,)), ((), ()))
    tn = (((0,), (0,)), ((), ()))
    for g in range(groups):
        lanes = slice(g * head_cols, (g + 1) * head_cols)
        q = queries[0, 0, :, lanes]
        grad = jnp.where(row_keep, grads[0, 0, :, lanes].astype(F32), 0.0).astype(BF16)
        keys = spread(rows_in[g, :, :head_cols])
        values = spread(rows_in[g, :, head_cols:])
        scores = lax.dot_general(keys, q, nt, preferred_element_type=F32) * scaling
        scores = scores.reshape(heads, source_rows, target_rows)
        scores = jnp.where(key_valid, scores, masked_score)
        shifted = jnp.exp(scores - jnp.max(scores, axis=1, keepdims=True))
        attention = shifted / jnp.sum(shifted, axis=1, keepdims=True)
        attention_bf = attention.reshape(span, target_rows).astype(BF16)
        out = lax.dot_general(attention_bf, values, tn, preferred_element_type=F32)
        context[0, 0, :, lanes] = jnp.where(row_keep, out, 0.0).astype(BF16)
        grad_values = jnp.dot(attention_bf, grad, preferred_element_type=F32)
        grad_attention = lax.dot_general(values, grad, nt, preferred_element_type=F32)
        grad_attention = grad_attention.reshape(heads, source_rows, target_rows)
        row_dot = jnp.sum(attention * grad_attention, axis=1, keepdims=True)
        grad_scores = attention * (grad_attention - row_dot)
        grad_scores = grad_scores.reshape(span, target_rows).astype(BF16)
        out = lax.dot_general(grad_scores, keys, tn, preferred_element_type=F32)
        grad_queries[0, 0, :, lanes] = (out * scaling).astype(BF16)
        grad_keys = jnp.dot(grad_scores, q, preferred_element_type=F32) * scaling
        grad_rows[g, :, :head_cols] = gather(grad_keys).astype(BF16)
        grad_rows[g, :, head_cols:] = gather(grad_values).astype(BF16)


def reduce_kernel(
    langs, shards, slots,
    grad_rows, facts, key_weight, value_weight,
    grad_memory, all_rows,
    weights, partial, first, paired, second, returning, third,
    weight_sem, a_send, a_recv, f_send, f_recv, p_send, p_recv, z_send, z_recv,
):
    lang = lax.axis_index("lang")
    shard = lax.axis_index("shard")
    core = lax.rem(shard, 2)
    chip = shard // 2
    chips = shards // 2
    sibling = (lang, chip * 2 + 1 - core)
    rows = grad_memory.shape[0]
    cols = grad_memory.shape[1] // CHUNKS
    head_cols = key_weight.shape[1]
    block = slots * rows
    nt = (((1,), (1,)), ((), ()))

    loads = [
        pltpu.make_async_copy(key_weight, weights.at[:, 0:head_cols], weight_sem.at[0]),
        pltpu.make_async_copy(
            value_weight, weights.at[:, head_cols : 2 * head_cols], weight_sem.at[1]
        ),
    ]
    for load in loads:
        load.start()
    enter(lang, shard, langs, shards)
    exchange(lang, shard, shards, grad_rows, all_rows, a_send, a_recv)
    for load in loads:
        load.wait()

    sent = []
    f_copies = []
    chosen = selection(facts, lang, langs, slots)
    weigh = [[chosen[r][j].astype(F32) for j in range(langs)] for r in range(slots)]

    def project_back(c):
        product = lax.dot_general(
            all_rows[...].reshape(shards * block, 2 * head_cols),
            weights[c * cols : (c + 1) * cols, :],
            nt,
            preferred_element_type=F32,
        )
        product = product.astype(BF16).reshape(chips, 2, block, cols)
        partial[c, 0] = product[:, 0]
        partial[c, 1] = product[:, 1]
        copy = remote(
            partial.at[c, 1 - core], first.at[c], f_send.at[c], f_recv.at[c], sibling
        )
        copy.start()
        f_copies.append(copy)

    p_copies = []
    z_copies = []

    def send_pairs(c):
        f_copies[c].wait_recv()
        part = []
        for d in range(1, chips):
            other = lax.rem(chip + d, chips)
            pair = partial[c, core, other].astype(F32) + first[c, other].astype(F32)
            paired[c, d] = pair.astype(BF16)
            copy = remote(
                paired.at[c, d], second.at[c, d], p_send.at[c, d], p_recv.at[c, d],
                (lang, other * 2 + core),
            )
            copy.start()
            part.append(copy)
        p_copies.append(part)

    def send_back(c):
        value = partial[c, core, chip].astype(F32) + first[c, chip].astype(F32)
        for d in range(1, chips):
            p_copies[c][d - 1].wait_recv()
            value = value + second[c, d].astype(F32)
        value = value.astype(BF16).astype(F32)
        for j in range(langs):
            back = value[0:rows] * weigh[0][j]
            for r in range(1, slots):
                back = back + value[r * rows : (r + 1) * rows] * weigh[r][j]
            returning[c, j] = back.astype(BF16)
        part = []
        for d in range(1, langs):
            other = lax.rem(lang + d, langs)
            copy = remote(
                returning.at[c, other], third.at[c, d], z_send.at[c, d], z_recv.at[c, d],
                (other, shard),
            )
            copy.start()
            part.append(copy)
        z_copies.append(part)

    def finish(c):
        value = returning[c, lang].astype(F32)
        for d in range(1, langs):
            z_copies[c][d - 1].wait_recv()
            value = value + third[c, d].astype(F32)
        grad_memory[:, c * cols : (c + 1) * cols] = value.astype(BF16)

    for turn in range(CHUNKS + 2):
        if turn < CHUNKS:
            project_back(turn)
        if 0 <= turn - 1 < CHUNKS:
            send_pairs(turn - 1)
        if 0 <= turn - 2:
            send_back(turn - 2)
    for c in range(CHUNKS):
        finish(c)
    sent += f_copies
    for c in range(CHUNKS):
        sent += p_copies[c] + z_copies[c]
    for copy in sent:
        copy.wait_send()


def weight_kernel(group, grads, grad_key, grad_value):
    head_cols = grad_key.shape[2]
    product = lax.dot_general(
        group[...], grads[...], (((0,), (0,)), ((), ())), preferred_element_type=F32
    )
    grad_key[0] = product[:, :head_cols].astype(BF16)
    grad_value[0] = product[:, head_cols:].astype(BF16)


def local(memory, lang_id, src_len, tgt_len, queries, key_weight, value_weight, grad_context):
    langs = lax.axis_size("lang")
    shards = lax.axis_size("shard")
    chips = shards // 2
    slots = queries.shape[1]
    target_rows = queries.shape[2]
    rows = memory.shape[1]
    width = memory.shape[2]
    head_cols = key_weight.shape[2]
    cols = width // CHUNKS
    block = slots * rows
    total_rows = shards * block
    vmem = pl.BlockSpec(memory_space=pltpu.VMEM)
    hbm = pl.BlockSpec(memory_space=pl.ANY)
    dma = pltpu.SemaphoreType.DMA
    keys = key_weight[0]
    values = value_weight[0]
    facts_in = jnp.concatenate([lang_id, src_len, tgt_len, jnp.zeros((5,), jnp.int32)])
    facts_in = jnp.broadcast_to(facts_in[:, None], (8, 128))

    group, rows_in, facts, lengths = pl.pallas_call(
        functools.partial(route_kernel, langs, shards, slots),
        out_shape=(
            jax.ShapeDtypeStruct((total_rows, width), BF16),
            jax.ShapeDtypeStruct((shards, block, 2 * head_cols), BF16),
            jax.ShapeDtypeStruct((langs, 8, 128), jnp.int32),
            jax.ShapeDtypeStruct((2 * slots, 128), jnp.int32),
        ),
        in_specs=[hbm, vmem, hbm, hbm],
        out_specs=(vmem, vmem, vmem, vmem),
        scratch_shapes=[
            pltpu.VMEM((langs, rows, width), BF16),
            pltpu.VMEM((width, 2 * head_cols), BF16),
            pltpu.VMEM((total_rows, 2 * head_cols), F32),
            pltpu.VMEM((shards, block, 2 * head_cols), BF16),
            dma((3,)),
            dma((langs,)),
            dma((langs,)),
            dma((langs, CHUNKS)),
            dma((langs, CHUNKS)),
            dma((chips, CHUNKS)),
            dma((chips, CHUNKS)),
            dma((chips, CHUNKS)),
            dma((chips, CHUNKS)),
            dma((shards,)),
            dma((shards,)),
        ],
        compiler_params=pltpu.CompilerParams(
            collective_id=0, has_side_effects=True, vmem_limit_bytes=VMEM_BYTES
        ),
        name="route_and_project",
    )(memory[0], facts_in, keys, values)

    per_step = max(1, min(shards, 2048 // head_cols))
    steps = shards // per_step
    wide = pl.BlockSpec(
        (1, 1, target_rows, per_step * head_cols), lambda r, p: (0, r, 0, p)
    )
    narrow = pl.BlockSpec((per_step, rows, 2 * head_cols), lambda r, p: (p, r, 0))
    context, grad_queries, grad_rows = pl.pallas_call(
        attend_kernel,
        grid=(slots, steps),
        out_shape=(
            jax.ShapeDtypeStruct(queries.shape, BF16),
            jax.ShapeDtypeStruct(queries.shape, BF16),
            jax.ShapeDtypeStruct(rows_in.shape, BF16),
        ),
        in_specs=[
            pl.BlockSpec((2 * slots, 128), lambda r, p: (0, 0)), wide, wide, narrow
        ],
        out_specs=(wide, wide, narrow),
        compiler_params=pltpu.CompilerParams(vmem_limit_bytes=VMEM_BYTES),
        name="attend_both_ways",
    )(lengths, queries, grad_context, rows_in)

    grad_memory, all_rows = pl.pallas_call(
        functools.partial(reduce_kernel, langs, shards, slots),
        out_shape=(
            jax.ShapeDtypeStruct((rows, width), BF16),
            jax.ShapeDtypeStruct((shards, block, 2 * head_cols), BF16),
        ),
        in_specs=[vmem, vmem, hbm, hbm],
        out_specs=(vmem, vmem),
        scratch_shapes=[
            pltpu.VMEM((width, 2 * head_cols), BF16),
            pltpu.VMEM((CHUNKS, 2, chips, block, cols), BF16),
            pltpu.VMEM((CHUNKS, chips, block, cols), BF16),
            pltpu.VMEM((CHUNKS, chips, block, cols), BF16),
            pltpu.VMEM((CHUNKS, chips, block, cols), BF16),
            pltpu.VMEM((CHUNKS, langs, rows, cols), BF16),
            pltpu.VMEM((CHUNKS, langs, rows, cols), BF16),
            dma((2,)),
            dma((shards,)),
            dma((shards,)),
            dma((CHUNKS,)),
            dma((CHUNKS,)),
            dma((CHUNKS, chips)),
            dma((CHUNKS, chips)),
            dma((CHUNKS, langs)),
            dma((CHUNKS, langs)),
        ],
        compiler_params=pltpu.CompilerParams(
            collective_id=1, has_side_effects=True, vmem_limit_bytes=VMEM_BYTES
        ),
        name="reduce_and_return",
    )(grad_rows, facts, keys, values)

    flat = all_rows.reshape(total_rows, 2 * head_cols)
    tile = width // 8
    out_tile = pl.BlockSpec((1, tile, head_cols), lambda i: (0, i, 0))
    grad_key, grad_value = pl.pallas_call(
        weight_kernel,
        grid=(8,),
        out_shape=(
            jax.ShapeDtypeStruct(key_weight.shape, BF16),
            jax.ShapeDtypeStruct(value_weight.shape, BF16),
        ),
        in_specs=[
            pl.BlockSpec((total_rows, tile), lambda i: (0, i)),
            pl.BlockSpec((total_rows, 2 * head_cols), lambda i: (0, 0)),
        ],
        out_specs=(out_tile, out_tile),
        compiler_params=pltpu.CompilerParams(vmem_limit_bytes=VMEM_BYTES),
        name="weight_gradients",
    )(group, flat)
    return (
        context,
        grad_queries,
        grad_memory[None],
        grad_key,
        grad_value,
    )


def solution(mesh):
    return jax.shard_map(
        local,
        mesh=mesh,
        in_specs=(
            P(("lang", "shard"), None, None),
            P(("lang", "shard")),
            P(("lang", "shard")),
            P(("lang", "shard")),
            P("lang", "shard", None, None),
            P("lang", None, "shard"),
            P("lang", None, "shard"),
            P("lang", "shard", None, None),
        ),
        out_specs=(
            P("lang", "shard", None, None),
            P("lang", "shard", None, None),
            P(("lang", "shard"), None, None),
            P("lang", None, "shard"),
            P("lang", None, "shard"),
        ),
        check_vma=False,
    )
```

```python
import functools

import jax
import jax.numpy as jnp
from jax import lax
from jax.experimental import pallas as pl
from jax.experimental.pallas import tpu as pltpu
from jax.sharding import PartitionSpec as P

HEAD = 128
CHUNKS = 4
AHEAD = 2
VMEM_BYTES = 50 * 1024 * 1024

masked_score = -1e30
MESH = pl.DeviceIdType.MESH
F32 = jnp.float32
BF16 = jnp.bfloat16


def remote(src, dst, send_sem, recv_sem, device):
    return pltpu.make_async_remote_copy(
        src_ref=src,
        dst_ref=dst,
        send_sem=send_sem,
        recv_sem=recv_sem,
        device_id=device,
        device_id_type=MESH,
    )


def enter(lang, shard, langs, shards):
    barrier = pltpu.get_barrier_semaphore()
    for step in range(1, langs):
        pl.semaphore_signal(
            barrier, inc=1, device_id=(lax.rem(lang + step, langs), shard), device_id_type=MESH
        )
    for step in range(1, shards):
        pl.semaphore_signal(
            barrier, inc=1, device_id=(lang, lax.rem(shard + step, shards)), device_id_type=MESH
        )
    pl.semaphore_wait(barrier, langs + shards - 2)


def selection(facts, lang, langs, slots):
    ids = [facts[j, 0:1, 0:1] for j in range(langs)]
    chosen = [[None] * langs for _ in range(slots)]
    for j in range(langs):
        rank = jnp.zeros((1, 1), jnp.int32)
        for k in range(j):
            rank = rank + jnp.where(ids[k] == ids[j], 1, 0)
        here = ids[j] == lang
        for r in range(slots):
            chosen[r][j] = jnp.where(here & (rank == r), 1, 0)
    return chosen


def attend(owners, lengths, queries, grads, rows_in, context, grad_queries, grad_rows):
    slots, target_rows = queries.shape[:2]
    head_cols = rows_in.shape[2] // 2
    source_rows = rows_in.shape[1] // slots
    heads = head_cols // HEAD
    span = heads * source_rows
    scaling = HEAD ** (-0.5)
    same = (
        lax.broadcasted_iota(jnp.int32, (span, head_cols), 0) // source_rows
        == lax.broadcasted_iota(jnp.int32, (span, head_cols), 1) // HEAD
    )
    positions = lax.broadcasted_iota(jnp.int32, (heads, source_rows, target_rows), 1)
    targets = lax.broadcasted_iota(jnp.int32, (target_rows, head_cols), 0)

    def spread(rows):
        wide = jnp.concatenate([rows] * heads, axis=0) if heads > 1 else rows
        return jnp.where(same, wide.astype(F32), 0.0).astype(BF16)

    def gather(wide):
        return jnp.concatenate(
            [
                wide[h * source_rows : (h + 1) * source_rows, h * HEAD : (h + 1) * HEAD]
                for h in range(heads)
            ],
            axis=1,
        )

    nt = (((1,), (1,)), ((), ()))
    tn = (((0,), (0,)), ((), ()))
    for owner, slot in [(owner, slot) for owner in owners for slot in range(slots)]:
        lanes = pl.ds(pl.multiple_of(owner * head_cols, HEAD), head_cols)
        near = slice(slot * source_rows, (slot + 1) * source_rows)
        src = jnp.maximum(lengths[slot : slot + 1, 0:1], 1).reshape(1, 1, 1)
        key_valid = positions < src
        row_keep = targets < lengths[slots + slot : slots + slot + 1, 0:1]
        q = queries[slot, :, lanes]
        grad = jnp.where(row_keep, grads[slot, :, lanes].astype(F32), 0.0).astype(BF16)
        keys = spread(rows_in[owner, near, :head_cols])
        values = spread(rows_in[owner, near, head_cols:])
        scores = lax.dot_general(keys, q, nt, preferred_element_type=F32) * scaling
        scores = scores.reshape(heads, source_rows, target_rows)
        scores = jnp.where(key_valid, scores, masked_score)
        shifted = jnp.exp(scores - jnp.max(scores, axis=1, keepdims=True))
        attention = shifted / jnp.sum(shifted, axis=1, keepdims=True)
        attention_bf = attention.reshape(span, target_rows).astype(BF16)
        out = lax.dot_general(attention_bf, values, tn, preferred_element_type=F32)
        context[slot, :, lanes] = jnp.where(row_keep, out, 0.0).astype(BF16)
        grad_values = jnp.dot(attention_bf, grad, preferred_element_type=F32)
        grad_attention = lax.dot_general(values, grad, nt, preferred_element_type=F32)
        grad_attention = grad_attention.reshape(heads, source_rows, target_rows)
        row_dot = jnp.sum(attention * grad_attention, axis=1, keepdims=True)
        grad_scores = attention * (grad_attention - row_dot)
        grad_scores = grad_scores.reshape(span, target_rows).astype(BF16)
        out = lax.dot_general(grad_scores, keys, tn, preferred_element_type=F32)
        grad_queries[slot, :, lanes] = (out * scaling).astype(BF16)
        grad_keys = jnp.dot(grad_scores, q, preferred_element_type=F32) * scaling
        grad_rows[owner, near, :head_cols] = gather(grad_keys).astype(BF16)
        grad_rows[owner, near, head_cols:] = gather(grad_values).astype(BF16)


def whole_kernel(
    langs, shards, slots,
    memory, facts_in, key_weight, value_weight, queries_in, grads_in,
    group, context, grad_queries, grad_memory, all_rows,
    facts, lengths, queries, grads, rows_in, grad_rows,
    column, weights, total, outgoing,
    partial, first, paired, second, returning, third,
    weight_sem, fact_send, fact_recv, z_send, z_recv,
    p_send, p_recv, s_send, s_recv, a_send, a_recv,
    b_send, b_recv, f_send, f_recv, q_send, q_recv, y_send, y_recv,
):
    lang = lax.axis_index("lang")
    shard = lax.axis_index("shard")
    core = lax.rem(shard, 2)
    chip = shard // 2
    chips = shards // 2
    sibling = (lang, chip * 2 + 1 - core)
    rows = memory.shape[0]
    width = memory.shape[1]
    cols = width // CHUNKS
    head_cols = key_weight.shape[1]
    block = slots * rows

    loads = [
        pltpu.make_async_copy(key_weight, weights.at[:, 0:head_cols], weight_sem.at[0]),
        pltpu.make_async_copy(
            value_weight, weights.at[:, head_cols : 2 * head_cols], weight_sem.at[1]
        ),
    ]
    for load in loads:
        load.start()
    tensors = [
        pltpu.make_async_copy(queries_in, queries, weight_sem.at[3]),
        pltpu.make_async_copy(grads_in, grads, weight_sem.at[4]),
    ]
    for load in tensors:
        load.start()
    enter(lang, shard, langs, shards)

    sent = []
    fact_copies = []
    for d in range(1, langs):
        copy = remote(
            facts_in, facts.at[lang], fact_send.at[d], fact_recv.at[d],
            (lax.rem(lang + d, langs), shard),
        )
        copy.start()
        fact_copies.append(copy)
    z_copies = []

    def start_z(c):
        part = []
        for d in range(1, langs):
            copy = remote(
                memory.at[:, c * cols : (c + 1) * cols],
                column.at[lang, :, c * cols : (c + 1) * cols],
                z_send.at[d, c], z_recv.at[d, c],
                (lax.rem(lang + d, langs), shard),
            )
            copy.start()
            part.append(copy)
        z_copies.append(part)

    for c in range(min(AHEAD, CHUNKS)):
        start_z(c)
    facts[lang] = facts_in[...]
    own = pltpu.make_async_copy(memory, column.at[lang], weight_sem.at[2])
    own.start()
    own.wait()
    for copy in fact_copies:
        copy.wait_recv()
    sent += fact_copies
    chosen = selection(facts, lang, langs, slots)
    for r in range(slots):
        for row, base in ((1, 0), (2, slots)):
            value = jnp.zeros((1, 1), jnp.int32)
            for j in range(langs):
                value = value + chosen[r][j] * facts[j, row : row + 1, 0:1]
            lengths[base + r : base + r + 1, :] = jnp.broadcast_to(value, (1, 128))
    weigh = [[chosen[r][j].astype(F32) for j in range(langs)] for r in range(slots)]

    def window(who, c):
        return group.at[pl.ds(pl.multiple_of(who * block, block), block), c * cols : (c + 1) * cols]

    p_copies = []
    s_copies = []

    def route(c):
        for copy in z_copies[c]:
            copy.wait_recv()
        sent.extend(z_copies[c])
        if c + AHEAD < CHUNKS:
            start_z(c + AHEAD)
        for r in range(slots):
            value = jnp.zeros((rows, cols), F32)
            for j in range(langs):
                value = value + column[j, :, c * cols : (c + 1) * cols].astype(F32) * weigh[r][j]
            start = pl.multiple_of(shard * block + r * rows, rows)
            group[pl.ds(start, rows), c * cols : (c + 1) * cols] = value.astype(BF16)
        part = []
        for d in range(1, chips):
            target = lax.rem(chip + d, chips) * 2 + core
            copy = remote(
                window(shard, c), window(shard, c), p_send.at[d, c], p_recv.at[d, c],
                (lang, target),
            )
            copy.start()
            part.append(copy)
        p_copies.append(part)
        copy = remote(window(shard, c), window(shard, c), s_send.at[0, c], s_recv.at[0, c], sibling)
        copy.start()
        s_copies.append([copy])

    def forward(c):
        for d in range(1, chips):
            p_copies[c][d - 1].wait_recv()
            source = lax.rem(chip + chips - d, chips) * 2 + core
            copy = remote(
                window(source, c), window(source, c), s_send.at[d, c], s_recv.at[d, c], sibling
            )
            copy.start()
            s_copies[c].append(copy)
        sent.extend(p_copies[c])

    def project(c):
        for copy in s_copies[c]:
            copy.wait_recv()
        sent.extend(s_copies[c])
        product = jnp.dot(
            group[:, c * cols : (c + 1) * cols],
            weights[c * cols : (c + 1) * cols, :],
            preferred_element_type=F32,
        )
        if c == 0:
            total[...] = product
        elif c < CHUNKS - 1:
            total[...] += product
        else:
            product = total[...] + product
            outgoing[...] = product.astype(BF16).reshape(outgoing.shape)

    for turn in range(CHUNKS + 2):
        if turn < CHUNKS:
            route(turn)
        if 0 <= turn - 1 < CHUNKS:
            forward(turn - 1)
        if turn == 2:
            for load in loads:
                load.wait()
        if 0 <= turn - 2:
            project(turn - 2)

    def bring(d):
        return remote(
            outgoing.at[lax.rem(shard + d, shards)], rows_in.at[shard],
            a_send.at[d], a_recv.at[d], (lang, lax.rem(shard + d, shards)),
        )

    def give(d):
        owner = lax.rem(shard + shards - d, shards)
        return remote(
            grad_rows.at[owner], all_rows.at[shard], b_send.at[d], b_recv.at[d], (lang, owner)
        )

    def start_bring(d, carry):
        bring(d).start()
        return carry

    def end_bring(d, carry):
        bring(d).wait_send()
        return carry

    def end_give(d, carry):
        give(d).wait_recv()
        give(d).wait_send()
        return carry

    lax.fori_loop(1, shards, start_bring, 0)
    rows_in[shard] = outgoing[shard]
    for load in tensors:
        load.wait()
    state = (lengths, queries, grads, rows_in, context, grad_queries, grad_rows)

    def attend_pair(step, carry):
        for d in (2 * step, 2 * step + 1):
            bring(d).wait_recv()
        attend([lax.rem(shard + shards - d, shards) for d in (2 * step, 2 * step + 1)], *state)
        for d in (2 * step, 2 * step + 1):
            give(d).start()
        return carry

    bring(1).wait_recv()
    attend([shard, lax.rem(shard + shards - 1, shards)], *state)
    give(1).start()
    all_rows[shard] = grad_rows[shard]
    lax.fori_loop(1, shards // 2, attend_pair, 0)
    lax.fori_loop(1, shards, end_give, 0)
    lax.fori_loop(1, shards, end_bring, 0)
    nt = (((1,), (1,)), ((), ()))
    f_copies = []

    def project_back(c):
        product = lax.dot_general(
            all_rows[...].reshape(shards * block, 2 * head_cols),
            weights[c * cols : (c + 1) * cols, :],
            nt,
            preferred_element_type=F32,
        )
        product = product.astype(BF16).reshape(chips, 2, block, cols)
        partial[c, 0] = product[:, 0]
        partial[c, 1] = product[:, 1]
        copy = remote(
            partial.at[c, 1 - core], first.at[c], f_send.at[c], f_recv.at[c], sibling
        )
        copy.start()
        f_copies.append(copy)

    p_copies = []
    z_copies = []

    def send_pairs(c):
        f_copies[c].wait_recv()
        part = []
        for d in range(1, chips):
            other = lax.rem(chip + d, chips)
            pair = partial[c, core, other].astype(F32) + first[c, other].astype(F32)
            paired[c, d] = pair.astype(BF16)
            copy = remote(
                paired.at[c, d], second.at[c, d], q_send.at[c, d], q_recv.at[c, d],
                (lang, other * 2 + core),
            )
            copy.start()
            part.append(copy)
        p_copies.append(part)

    def send_back(c):
        value = partial[c, core, chip].astype(F32) + first[c, chip].astype(F32)
        for d in range(1, chips):
            p_copies[c][d - 1].wait_recv()
            value = value + second[c, d].astype(F32)
        value = value.astype(BF16).astype(F32)
        for j in range(langs):
            back = value[0:rows] * weigh[0][j]
            for r in range(1, slots):
                back = back + value[r * rows : (r + 1) * rows] * weigh[r][j]
            returning[c, j] = back.astype(BF16)
        part = []
        for d in range(1, langs):
            other = lax.rem(lang + d, langs)
            copy = remote(
                returning.at[c, other], third.at[c, d], y_send.at[c, d], y_recv.at[c, d],
                (other, shard),
            )
            copy.start()
            part.append(copy)
        z_copies.append(part)

    def finish(c):
        value = returning[c, lang].astype(F32)
        for d in range(1, langs):
            z_copies[c][d - 1].wait_recv()
            value = value + third[c, d].astype(F32)
        grad_memory[:, c * cols : (c + 1) * cols] = value.astype(BF16)

    for turn in range(CHUNKS + 2):
        if turn < CHUNKS:
            project_back(turn)
        if 0 <= turn - 1 < CHUNKS:
            send_pairs(turn - 1)
        if 0 <= turn - 2:
            send_back(turn - 2)
    for c in range(CHUNKS):
        finish(c)
    sent += f_copies
    for c in range(CHUNKS):
        sent += p_copies[c] + z_copies[c]
    for copy in sent:
        copy.wait_send()


def weight_kernel(group, grads, grad_key, grad_value):
    head_cols = grad_key.shape[2]
    product = lax.dot_general(
        group[...], grads[...], (((0,), (0,)), ((), ())), preferred_element_type=F32
    )
    grad_key[0] = product[:, :head_cols].astype(BF16)
    grad_value[0] = product[:, head_cols:].astype(BF16)


def local(memory, lang_id, src_len, tgt_len, queries, key_weight, value_weight, grad_context):
    langs = lax.axis_size("lang")
    shards = lax.axis_size("shard")
    chips = shards // 2
    slots = queries.shape[1]
    target_rows = queries.shape[2]
    rows = memory.shape[1]
    width = memory.shape[2]
    head_cols = key_weight.shape[2]
    cols = width // CHUNKS
    block = slots * rows
    total_rows = shards * block
    vmem = pl.BlockSpec(memory_space=pltpu.VMEM)
    hbm = pl.BlockSpec(memory_space=pl.ANY)
    dma = pltpu.SemaphoreType.DMA
    keys = key_weight[0]
    values = value_weight[0]
    facts_in = jnp.concatenate([lang_id, src_len, tgt_len, jnp.zeros((5,), jnp.int32)])
    facts_in = jnp.broadcast_to(facts_in[:, None], (8, 128))

    three = jax.ShapeDtypeStruct((shards, block, 2 * head_cols), BF16)
    tensor = jax.ShapeDtypeStruct(queries.shape[1:], BF16)
    three_vmem = pltpu.VMEM(three.shape, BF16)
    tensor_vmem = pltpu.VMEM(tensor.shape, BF16)
    pairs_vmem = pltpu.VMEM((CHUNKS, chips, block, cols), BF16)
    back_vmem = pltpu.VMEM((CHUNKS, langs, rows, cols), BF16)
    group, context, grad_queries, grad_memory, all_rows = pl.pallas_call(
        functools.partial(whole_kernel, langs, shards, slots),
        out_shape=(
            jax.ShapeDtypeStruct((total_rows, width), BF16),
            tensor,
            tensor,
            jax.ShapeDtypeStruct((rows, width), BF16),
            three,
        ),
        in_specs=[hbm, vmem, hbm, hbm, hbm, hbm],
        out_specs=(vmem, vmem, vmem, vmem, vmem),
        scratch_shapes=[
            pltpu.VMEM((langs, 8, 128), jnp.int32),
            pltpu.VMEM((2 * slots, 128), jnp.int32),
            tensor_vmem,
            tensor_vmem,
            three_vmem,
            three_vmem,
            pltpu.VMEM((langs, rows, width), BF16),
            pltpu.VMEM((width, 2 * head_cols), BF16),
            pltpu.VMEM((total_rows, 2 * head_cols), F32),
            three_vmem,
            pltpu.VMEM((CHUNKS, 2, chips, block, cols), BF16),
            pairs_vmem,
            pairs_vmem,
            pairs_vmem,
            back_vmem,
            back_vmem,
            dma((5,)),
            dma((langs,)),
            dma((langs,)),
            dma((langs, CHUNKS)),
            dma((langs, CHUNKS)),
            dma((chips, CHUNKS)),
            dma((chips, CHUNKS)),
            dma((chips, CHUNKS)),
            dma((chips, CHUNKS)),
            dma((shards,)),
            dma((shards,)),
            dma((shards,)),
            dma((shards,)),
            dma((CHUNKS,)),
            dma((CHUNKS,)),
            dma((CHUNKS, chips)),
            dma((CHUNKS, chips)),
            dma((CHUNKS, langs)),
            dma((CHUNKS, langs)),
        ],
        compiler_params=pltpu.CompilerParams(
            collective_id=0, has_side_effects=True, vmem_limit_bytes=VMEM_BYTES
        ),
        name="route_attend_reduce",
    )(memory[0], facts_in, keys, values, queries[0], grad_context[0])

    flat = all_rows.reshape(total_rows, 2 * head_cols)
    tile = width // 8
    out_tile = pl.BlockSpec((1, tile, head_cols), lambda i: (0, i, 0))
    grad_key, grad_value = pl.pallas_call(
        weight_kernel,
        grid=(8,),
        out_shape=(
            jax.ShapeDtypeStruct(key_weight.shape, BF16),
            jax.ShapeDtypeStruct(value_weight.shape, BF16),
        ),
        in_specs=[
            pl.BlockSpec((total_rows, tile), lambda i: (0, i)),
            pl.BlockSpec((total_rows, 2 * head_cols), lambda i: (0, 0)),
        ],
        out_specs=(out_tile, out_tile),
        compiler_params=pltpu.CompilerParams(vmem_limit_bytes=VMEM_BYTES),
        name="weight_gradients",
    )(group, flat)
    return (
        context[None],
        grad_queries[None],
        grad_memory[None],
        grad_key,
        grad_value,
    )


def solution(mesh):
    return jax.shard_map(
        local,
        mesh=mesh,
        in_specs=(
            P(("lang", "shard"), None, None),
            P(("lang", "shard")),
            P(("lang", "shard")),
            P(("lang", "shard")),
            P("lang", "shard", None, None),
            P("lang", None, "shard"),
            P("lang", None, "shard"),
            P("lang", "shard", None, None),
        ),
        out_specs=(
            P("lang", "shard", None, None),
            P("lang", "shard", None, None),
            P(("lang", "shard"), None, None),
            P("lang", None, "shard"),
            P("lang", None, "shard"),
        ),
        check_vma=False,
    )
```

```python
import functools

import jax
import jax.numpy as jnp
from jax import lax
from jax.experimental import pallas as pl
from jax.experimental.pallas import tpu as pltpu
from jax.sharding import PartitionSpec as P

HEAD = 128
CHUNKS = 4
AHEAD = 2
VMEM_BYTES = 50 * 1024 * 1024

masked_score = -1e30
MESH = pl.DeviceIdType.MESH
F32 = jnp.float32
BF16 = jnp.bfloat16


def remote(src, dst, send_sem, recv_sem, device):
    return pltpu.make_async_remote_copy(
        src_ref=src,
        dst_ref=dst,
        send_sem=send_sem,
        recv_sem=recv_sem,
        device_id=device,
        device_id_type=MESH,
    )


def enter(lang, shard, langs, shards):
    barrier = pltpu.get_barrier_semaphore()
    for step in range(1, langs):
        pl.semaphore_signal(
            barrier, inc=1, device_id=(lax.rem(lang + step, langs), shard), device_id_type=MESH
        )
    for step in range(1, shards):
        pl.semaphore_signal(
            barrier, inc=1, device_id=(lang, lax.rem(shard + step, shards)), device_id_type=MESH
        )
    pl.semaphore_wait(barrier, langs + shards - 2)


def selection(facts, lang, langs, slots):
    ids = [facts[j, 0:1, 0:1] for j in range(langs)]
    chosen = [[None] * langs for _ in range(slots)]
    for j in range(langs):
        rank = jnp.zeros((1, 1), jnp.int32)
        for k in range(j):
            rank = rank + jnp.where(ids[k] == ids[j], 1, 0)
        here = ids[j] == lang
        for r in range(slots):
            chosen[r][j] = jnp.where(here & (rank == r), 1, 0)
    return chosen


def attend(owners, lengths, queries, grads, rows_in, context, grad_queries, grad_rows):
    slots, target_rows = queries.shape[:2]
    head_cols = rows_in.shape[2] // 2
    source_rows = rows_in.shape[1] // slots
    heads = head_cols // HEAD
    span = heads * source_rows
    scaling = HEAD ** (-0.5)
    same = (
        lax.broadcasted_iota(jnp.int32, (span, head_cols), 0) // source_rows
        == lax.broadcasted_iota(jnp.int32, (span, head_cols), 1) // HEAD
    )
    positions = lax.broadcasted_iota(jnp.int32, (heads, source_rows, target_rows), 1)
    targets = lax.broadcasted_iota(jnp.int32, (target_rows, head_cols), 0)

    def spread(rows):
        wide = jnp.concatenate([rows] * heads, axis=0) if heads > 1 else rows
        return jnp.where(same, wide.astype(F32), 0.0).astype(BF16)

    def gather(wide):
        return jnp.concatenate(
            [
                wide[h * source_rows : (h + 1) * source_rows, h * HEAD : (h + 1) * HEAD]
                for h in range(heads)
            ],
            axis=1,
        )

    nt = (((1,), (1,)), ((), ()))
    tn = (((0,), (0,)), ((), ()))
    for owner, slot in [(owner, slot) for owner in owners for slot in range(slots)]:
        lanes = pl.ds(pl.multiple_of(owner * head_cols, HEAD), head_cols)
        near = slice(slot * source_rows, (slot + 1) * source_rows)
        src = jnp.maximum(lengths[slot : slot + 1, 0:1], 1).reshape(1, 1, 1)
        key_valid = positions < src
        row_keep = targets < lengths[slots + slot : slots + slot + 1, 0:1]
        q = queries[slot, :, lanes]
        grad = jnp.where(row_keep, grads[slot, :, lanes].astype(F32), 0.0).astype(BF16)
        keys = spread(rows_in[owner, near, :head_cols])
        values = spread(rows_in[owner, near, head_cols:])
        scores = lax.dot_general(keys, q, nt, preferred_element_type=F32) * scaling
        scores = scores.reshape(heads, source_rows, target_rows)
        scores = jnp.where(key_valid, scores, masked_score)
        shifted = jnp.exp(scores - jnp.max(scores, axis=1, keepdims=True))
        attention = shifted / jnp.sum(shifted, axis=1, keepdims=True)
        attention_bf = attention.reshape(span, target_rows).astype(BF16)
        out = lax.dot_general(attention_bf, values, tn, preferred_element_type=F32)
        context[slot, :, lanes] = jnp.where(row_keep, out, 0.0).astype(BF16)
        grad_values = jnp.dot(attention_bf, grad, preferred_element_type=F32)
        grad_attention = lax.dot_general(values, grad, nt, preferred_element_type=F32)
        grad_attention = grad_attention.reshape(heads, source_rows, target_rows)
        row_dot = jnp.sum(attention * grad_attention, axis=1, keepdims=True)
        grad_scores = attention * (grad_attention - row_dot)
        grad_scores = grad_scores.reshape(span, target_rows).astype(BF16)
        out = lax.dot_general(grad_scores, keys, tn, preferred_element_type=F32)
        grad_queries[slot, :, lanes] = (out * scaling).astype(BF16)
        grad_keys = jnp.dot(grad_scores, q, preferred_element_type=F32) * scaling
        grad_rows[owner, near, :head_cols] = gather(grad_keys).astype(BF16)
        grad_rows[owner, near, head_cols:] = gather(grad_values).astype(BF16)


def whole_kernel(
    langs, shards, slots,
    memory, facts_in, key_weight, value_weight, queries_in, grads_in,
    group, context, grad_queries, grad_memory, all_rows,
    facts, lengths, queries, grads, rows_in, grad_rows,
    column, weights, total, outgoing,
    partial, first, paired, second, returning, third,
    weight_sem, fact_send, fact_recv, z_send, z_recv,
    p_send, p_recv, s_send, s_recv, a_send, a_recv,
    b_send, b_recv, f_send, f_recv, q_send, q_recv, y_send, y_recv,
):
    lang = lax.axis_index("lang")
    shard = lax.axis_index("shard")
    core = lax.rem(shard, 2)
    chip = shard // 2
    chips = shards // 2
    sibling = (lang, chip * 2 + 1 - core)
    rows = memory.shape[0]
    width = memory.shape[1]
    cols = width // CHUNKS
    head_cols = key_weight.shape[1]
    block = slots * rows

    loads = [
        pltpu.make_async_copy(key_weight, weights.at[:, 0:head_cols], weight_sem.at[0]),
        pltpu.make_async_copy(
            value_weight, weights.at[:, head_cols : 2 * head_cols], weight_sem.at[1]
        ),
    ]
    for load in loads:
        load.start()
    tensors = [
        pltpu.make_async_copy(queries_in, queries, weight_sem.at[3]),
        pltpu.make_async_copy(grads_in, grads, weight_sem.at[4]),
    ]
    for load in tensors:
        load.start()
    enter(lang, shard, langs, shards)

    sent = []
    fact_copies = []
    for d in range(1, langs):
        copy = remote(
            facts_in, facts.at[lang], fact_send.at[d], fact_recv.at[d],
            (lax.rem(lang + d, langs), shard),
        )
        copy.start()
        fact_copies.append(copy)
    z_copies = []

    def start_z(c):
        part = []
        for d in range(1, langs):
            copy = remote(
                memory.at[:, c * cols : (c + 1) * cols],
                column.at[lang, :, c * cols : (c + 1) * cols],
                z_send.at[d, c], z_recv.at[d, c],
                (lax.rem(lang + d, langs), shard),
            )
            copy.start()
            part.append(copy)
        z_copies.append(part)

    for c in range(min(AHEAD, CHUNKS)):
        start_z(c)
    facts[lang] = facts_in[...]
    own = pltpu.make_async_copy(memory, column.at[lang], weight_sem.at[2])
    own.start()
    own.wait()
    for copy in fact_copies:
        copy.wait_recv()
    sent += fact_copies
    chosen = selection(facts, lang, langs, slots)
    for r in range(slots):
        for row, base in ((1, 0), (2, slots)):
            value = jnp.zeros((1, 1), jnp.int32)
            for j in range(langs):
                value = value + chosen[r][j] * facts[j, row : row + 1, 0:1]
            lengths[base + r : base + r + 1, :] = jnp.broadcast_to(value, (1, 128))
    weigh = [[chosen[r][j].astype(F32) for j in range(langs)] for r in range(slots)]

    def window(who, c):
        return group.at[pl.ds(pl.multiple_of(who * block, block), block), c * cols : (c + 1) * cols]

    p_copies = []
    s_copies = []

    def route(c):
        for copy in z_copies[c]:
            copy.wait_recv()
        sent.extend(z_copies[c])
        if c + AHEAD < CHUNKS:
            start_z(c + AHEAD)
        for r in range(slots):
            value = jnp.zeros((rows, cols), F32)
            for j in range(langs):
                value = value + column[j, :, c * cols : (c + 1) * cols].astype(F32) * weigh[r][j]
            start = pl.multiple_of(shard * block + r * rows, rows)
            group[pl.ds(start, rows), c * cols : (c + 1) * cols] = value.astype(BF16)
        part = []
        for d in range(1, chips):
            target = lax.rem(chip + d, chips) * 2 + core
            copy = remote(
                window(shard, c), window(shard, c), p_send.at[d, c], p_recv.at[d, c],
                (lang, target),
            )
            copy.start()
            part.append(copy)
        p_copies.append(part)
        copy = remote(window(shard, c), window(shard, c), s_send.at[0, c], s_recv.at[0, c], sibling)
        copy.start()
        s_copies.append([copy])

    def forward(c):
        for d in range(1, chips):
            p_copies[c][d - 1].wait_recv()
            source = lax.rem(chip + chips - d, chips) * 2 + core
            copy = remote(
                window(source, c), window(source, c), s_send.at[d, c], s_recv.at[d, c], sibling
            )
            copy.start()
            s_copies[c].append(copy)
        sent.extend(p_copies[c])

    def project(c):
        for copy in s_copies[c]:
            copy.wait_recv()
        sent.extend(s_copies[c])
        product = jnp.dot(
            group[:, c * cols : (c + 1) * cols],
            weights[c * cols : (c + 1) * cols, :],
            preferred_element_type=F32,
        )
        if c == 0:
            total[...] = product
        elif c < CHUNKS - 1:
            total[...] += product
        else:
            product = total[...] + product
            outgoing[...] = product.astype(BF16).reshape(outgoing.shape)

    for turn in range(CHUNKS + 2):
        if turn < CHUNKS:
            route(turn)
        if 0 <= turn - 1 < CHUNKS:
            forward(turn - 1)
        if turn == 2:
            for load in loads:
                load.wait()
        if 0 <= turn - 2:
            project(turn - 2)

    def bring(d):
        return remote(
            outgoing.at[lax.rem(shard + d, shards)], rows_in.at[shard],
            a_send.at[d], a_recv.at[d], (lang, lax.rem(shard + d, shards)),
        )

    def give(d):
        owner = lax.rem(shard + shards - d, shards)
        return remote(
            grad_rows.at[owner], all_rows.at[shard], b_send.at[d], b_recv.at[d], (lang, owner)
        )

    def start_bring(d, carry):
        bring(d).start()
        return carry

    def end_bring(d, carry):
        bring(d).wait_send()
        return carry

    def end_give(d, carry):
        give(d).wait_recv()
        give(d).wait_send()
        return carry

    lax.fori_loop(1, shards, start_bring, 0)
    rows_in[shard] = outgoing[shard]
    for load in tensors:
        load.wait()
    state = (lengths, queries, grads, rows_in, context, grad_queries, grad_rows)

    def attend_pair(step, carry):
        for d in (2 * step, 2 * step + 1):
            bring(d).wait_recv()
        attend([lax.rem(shard + shards - d, shards) for d in (2 * step, 2 * step + 1)], *state)
        for d in (2 * step, 2 * step + 1):
            give(d).start()
        return carry

    bring(1).wait_recv()
    attend([shard, lax.rem(shard + shards - 1, shards)], *state)
    give(1).start()
    all_rows[shard] = grad_rows[shard]
    lax.fori_loop(1, shards // 2, attend_pair, 0)
    lax.fori_loop(1, shards, end_give, 0)
    lax.fori_loop(1, shards, end_bring, 0)
    nt = (((1,), (1,)), ((), ()))
    f_copies = []

    def project_back(c):
        product = lax.dot_general(
            all_rows[...].reshape(shards * block, 2 * head_cols),
            weights[c * cols : (c + 1) * cols, :],
            nt,
            preferred_element_type=F32,
        )
        product = product.astype(BF16).reshape(chips, 2, block, cols)
        partial[c, 0] = product[:, 0]
        partial[c, 1] = product[:, 1]
        copy = remote(
            partial.at[c, 1 - core], first.at[c], f_send.at[c], f_recv.at[c], sibling
        )
        copy.start()
        f_copies.append(copy)

    p_copies = []
    z_copies = []

    def send_pairs(c):
        f_copies[c].wait_recv()
        part = []
        for d in range(1, chips):
            other = lax.rem(chip + d, chips)
            pair = partial[c, core, other].astype(F32) + first[c, other].astype(F32)
            paired[c, d] = pair.astype(BF16)
            copy = remote(
                paired.at[c, d], second.at[c, d], q_send.at[c, d], q_recv.at[c, d],
                (lang, other * 2 + core),
            )
            copy.start()
            part.append(copy)
        p_copies.append(part)

    def send_back(c):
        value = partial[c, core, chip].astype(F32) + first[c, chip].astype(F32)
        for d in range(1, chips):
            p_copies[c][d - 1].wait_recv()
            value = value + second[c, d].astype(F32)
        value = value.astype(BF16).astype(F32)
        for j in range(langs):
            back = value[0:rows] * weigh[0][j]
            for r in range(1, slots):
                back = back + value[r * rows : (r + 1) * rows] * weigh[r][j]
            returning[c, j] = back.astype(BF16)
        part = []
        for d in range(1, langs):
            other = lax.rem(lang + d, langs)
            copy = remote(
                returning.at[c, other], third.at[c, d], y_send.at[c, d], y_recv.at[c, d],
                (other, shard),
            )
            copy.start()
            part.append(copy)
        z_copies.append(part)

    def finish(c):
        value = returning[c, lang].astype(F32)
        for d in range(1, langs):
            z_copies[c][d - 1].wait_recv()
            value = value + third[c, d].astype(F32)
        grad_memory[:, c * cols : (c + 1) * cols] = value.astype(BF16)

    for turn in range(CHUNKS + 2):
        if turn < CHUNKS:
            project_back(turn)
        if 0 <= turn - 1 < CHUNKS:
            send_pairs(turn - 1)
        if 0 <= turn - 2:
            send_back(turn - 2)
    for c in range(CHUNKS):
        finish(c)
    sent += f_copies
    for c in range(CHUNKS):
        sent += p_copies[c] + z_copies[c]
    for copy in sent:
        copy.wait_send()


def weight_kernel(
    group, grads, context_in, queries_in, memory_in,
    grad_key, grad_value, context, grad_queries, grad_memory,
):
    context[...] = context_in[...]
    grad_queries[...] = queries_in[...]
    grad_memory[...] = memory_in[...]
    head_cols = grad_key.shape[2]
    product = lax.dot_general(
        group[...], grads[...], (((0,), (0,)), ((), ())), preferred_element_type=F32
    )
    grad_key[0] = product[:, :head_cols].astype(BF16)
    grad_value[0] = product[:, head_cols:].astype(BF16)


def local(memory, lang_id, src_len, tgt_len, queries, key_weight, value_weight, grad_context):
    langs = lax.axis_size("lang")
    shards = lax.axis_size("shard")
    chips = shards // 2
    slots = queries.shape[1]
    target_rows = queries.shape[2]
    rows = memory.shape[1]
    width = memory.shape[2]
    head_cols = key_weight.shape[2]
    cols = width // CHUNKS
    block = slots * rows
    total_rows = shards * block
    vmem = pl.BlockSpec(memory_space=pltpu.VMEM)
    hbm = pl.BlockSpec(memory_space=pl.ANY)
    dma = pltpu.SemaphoreType.DMA
    keys = key_weight[0]
    values = value_weight[0]
    facts_in = jnp.concatenate([lang_id, src_len, tgt_len, jnp.zeros((5,), jnp.int32)])
    facts_in = jnp.broadcast_to(facts_in[:, None], (8, 128))

    three = jax.ShapeDtypeStruct((shards, block, 2 * head_cols), BF16)
    tensor = jax.ShapeDtypeStruct(queries.shape[1:], BF16)
    three_vmem = pltpu.VMEM(three.shape, BF16)
    tensor_vmem = pltpu.VMEM(tensor.shape, BF16)
    pairs_vmem = pltpu.VMEM((CHUNKS, chips, block, cols), BF16)
    back_vmem = pltpu.VMEM((CHUNKS, langs, rows, cols), BF16)
    group, context, grad_queries, grad_memory, all_rows = pl.pallas_call(
        functools.partial(whole_kernel, langs, shards, slots),
        out_shape=(
            jax.ShapeDtypeStruct((total_rows, width), BF16),
            tensor,
            tensor,
            jax.ShapeDtypeStruct((rows, width), BF16),
            three,
        ),
        in_specs=[hbm, vmem, hbm, hbm, hbm, hbm],
        out_specs=(vmem, vmem, vmem, vmem, vmem),
        scratch_shapes=[
            pltpu.VMEM((langs, 8, 128), jnp.int32),
            pltpu.VMEM((2 * slots, 128), jnp.int32),
            tensor_vmem,
            tensor_vmem,
            three_vmem,
            three_vmem,
            pltpu.VMEM((langs, rows, width), BF16),
            pltpu.VMEM((width, 2 * head_cols), BF16),
            pltpu.VMEM((total_rows, 2 * head_cols), F32),
            three_vmem,
            pltpu.VMEM((CHUNKS, 2, chips, block, cols), BF16),
            pairs_vmem,
            pairs_vmem,
            pairs_vmem,
            back_vmem,
            back_vmem,
            dma((5,)),
            dma((langs,)),
            dma((langs,)),
            dma((langs, CHUNKS)),
            dma((langs, CHUNKS)),
            dma((chips, CHUNKS)),
            dma((chips, CHUNKS)),
            dma((chips, CHUNKS)),
            dma((chips, CHUNKS)),
            dma((shards,)),
            dma((shards,)),
            dma((shards,)),
            dma((shards,)),
            dma((CHUNKS,)),
            dma((CHUNKS,)),
            dma((CHUNKS, chips)),
            dma((CHUNKS, chips)),
            dma((CHUNKS, langs)),
            dma((CHUNKS, langs)),
        ],
        compiler_params=pltpu.CompilerParams(
            collective_id=0, has_side_effects=True, vmem_limit_bytes=VMEM_BYTES
        ),
        name="route_attend_reduce",
    )(memory[0], facts_in, keys, values, queries[0], grad_context[0])

    flat = all_rows.reshape(total_rows, 2 * head_cols)
    tile = width // 8
    out_tile = pl.BlockSpec((1, tile, head_cols), lambda i: (0, i, 0))
    tensor_tile = pl.BlockSpec((slots, target_rows, tile), lambda i: (0, 0, i))
    memory_tile = pl.BlockSpec((rows, tile), lambda i: (0, i))
    grad_key, grad_value, context, grad_queries, grad_memory = pl.pallas_call(
        weight_kernel,
        grid=(8,),
        out_shape=(
            jax.ShapeDtypeStruct(key_weight.shape, BF16),
            jax.ShapeDtypeStruct(value_weight.shape, BF16),
            tensor,
            tensor,
            jax.ShapeDtypeStruct((rows, width), BF16),
        ),
        in_specs=[
            pl.BlockSpec((total_rows, tile), lambda i: (0, i)),
            pl.BlockSpec((total_rows, 2 * head_cols), lambda i: (0, 0)),
            tensor_tile,
            tensor_tile,
            memory_tile,
        ],
        out_specs=(out_tile, out_tile, tensor_tile, tensor_tile, memory_tile),
        compiler_params=pltpu.CompilerParams(vmem_limit_bytes=VMEM_BYTES),
        name="weight_gradients",
    )(group, flat, context, grad_queries, grad_memory)
    return (
        context[None],
        grad_queries[None],
        grad_memory[None],
        grad_key,
        grad_value,
    )


def solution(mesh):
    return jax.shard_map(
        local,
        mesh=mesh,
        in_specs=(
            P(("lang", "shard"), None, None),
            P(("lang", "shard")),
            P(("lang", "shard")),
            P(("lang", "shard")),
            P("lang", "shard", None, None),
            P("lang", None, "shard"),
            P("lang", None, "shard"),
            P("lang", "shard", None, None),
        ),
        out_specs=(
            P("lang", "shard", None, None),
            P("lang", "shard", None, None),
            P(("lang", "shard"), None, None),
            P("lang", None, "shard"),
            P("lang", None, "shard"),
        ),
        check_vma=False,
    )
```
